256 devices in a mesh: grp: 4 (over z_hi, core), dev: 64 (over z_lo, y, x).
Axes of the slice: x: 4, y: 4, z: 8 (z_hi: 2, z_lo: 4; z = z_hi * 4 + z_lo), core: 2. Of those that a mesh axis runs over, the one named last changes fastest.
Arguments:
- key_tokens: bfloat16 [32768, 768], P(('grp', 'dev')), may hold values from -6 to 6
- value_tokens: bfloat16 [32768, 768], P(('grp', 'dev')), may hold values from -6 to 6
- queries: bfloat16 [32768, 768], P(('grp', 'dev')), may hold values from -192 to 192
- token_rate: float32 [32768], P(('grp', 'dev')), may hold values from 0.00019934 to 0.00159472
- fast_weights: bfloat16 [3, 1536, 768], P(None, ('grp', 'dev')), may hold values from -0.21875 to 0.21875
Outputs:
- target_out: bfloat16 [32768, 768], P(('grp', 'dev'))
The draws below stay inside these ranges and needn't reach their ends.
All inputs are finite; a program needn't handle non-finite values.
Results may differ from the reference program's by a relative error of at most 0.012.
The reference program's roundings to bfloat16 on the way count: a program that leaves them out, or rounds other values in their place, can miss the bound.
Values may be sent and summed in bfloat16 or wider, within the bound.
A program may use at most 64 MiB of HBM per device.

```python
import math
import jax
import jax.numpy as jnp
from jax import lax

D = 768
HID = 1536
HEADS = 12
HEAD_DIM = 64
TOK_DEV = 128
Q_DEV = 128
TOKENS = 32768
QUERIES = 32768


def drawn_pair(key):
    seeded = jax.random.fold_in(key, 7)
    first, second = jax.random.split(seeded, 2)
    block_count = TOKENS // TOK_DEV
    key_draw = jax.random.truncated_normal(first, -6.0, 6.0, (block_count, TOK_DEV, D), jnp.float32)
    query_draw = jax.random.truncated_normal(second, -6.0, 6.0, (block_count, Q_DEV, D), jnp.float32)
    return (key_draw.reshape(TOKENS, D), query_draw.reshape(QUERIES, D))


def draw_key_tokens(key, part):
    return drawn_pair(key)[0].astype(jnp.bfloat16)


def draw_queries(key, part):
    return drawn_pair(key)[1].astype(jnp.bfloat16)


def block_scale(key, shape, cuts, least, top_value):
    loudness, own = 1.0, jax.random.fold_in(key, 6)
    for axis_at, parts in cuts:
        steps = jnp.exp(jax.random.uniform(jax.random.fold_in(own, axis_at), (parts,), jnp.float32, least / len(cuts), top_value / len(cuts)))
        loudness = loudness * jnp.repeat(steps, shape[axis_at] // parts).reshape([-1 if axis == axis_at else 1 for axis in range(len(shape))])
    return loudness


def scatter_about(own_key, shape, spread, most, pieces=(), held_as=jnp.bfloat16):
    entries = spread * jax.random.normal(own_key, shape, jnp.float32)
    if pieces:
        entries = entries * block_scale(own_key, shape, pieces, -0.22, 0.18)
    return jnp.clip(entries, -most, most).astype(held_as)


def setup_inputs(seed: int = 0) -> dict:
    arg_keys = jax.random.split(jax.random.key(seed), 6)
    return {
        "key_tokens": draw_key_tokens(jax.random.fold_in(arg_keys[5], 71), 0),
        "value_tokens": scatter_about(arg_keys[1], (TOKENS, D), 1.0, 6.0, ((0, 256),)),
        "queries": draw_queries(jax.random.fold_in(arg_keys[5], 71), 0),
        "token_rate": jnp.clip(jnp.exp(math.log(0.00159472) - 2.0794415 * jax.random.uniform(arg_keys[3], (TOKENS,), jnp.float32) ** block_scale(arg_keys[3], (TOKENS,), ((0, 256),), -0.2, 0.2)), 0.00019934, 0.00159472),
        "fast_weights": scatter_about(arg_keys[4], (3, HID, D), D ** -0.5, 0.21875, ((1, 256),)),
    }


epsilon = 1e-06

def rms_rows(matrix):
    return matrix / jnp.sqrt(lax.optimization_barrier(jnp.mean(matrix * matrix, axis=-1, keepdims=True)) + epsilon)

def gradient_rows(weights, key_normed, signal):
    gate_act = jnp.dot(key_normed, weights[0].T, preferred_element_type=jnp.float32)
    up_act = jnp.dot(key_normed, weights[1].T, preferred_element_type=jnp.float32)
    sigmoid_gate = jax.nn.sigmoid(gate_act)
    silu_gate = gate_act * sigmoid_gate
    hidden_bf = (silu_gate * up_act).astype(jnp.bfloat16)
    down_grad = jnp.dot(hidden_bf.T, signal, preferred_element_type=jnp.float32)
    hidden_grad = jnp.dot(signal, weights[2].T, preferred_element_type=jnp.float32)
    gate_grad = (hidden_grad * up_act * sigmoid_gate * (1.0 + gate_act * (1.0 - sigmoid_gate))).astype(jnp.bfloat16)
    up_grad = (hidden_grad * silu_gate).astype(jnp.bfloat16)
    return jnp.stack([jnp.dot(gate_grad.T, key_normed, preferred_element_type=jnp.float32), jnp.dot(up_grad.T, key_normed, preferred_element_type=jnp.float32), down_grad])

def fast_apply(weights, query_normed):
    gate_act = jnp.dot(query_normed, weights[0].T, preferred_element_type=jnp.float32)
    up_act = jnp.dot(query_normed, weights[1].T, preferred_element_type=jnp.float32)
    hidden_bf = (jax.nn.silu(gate_act) * up_act).astype(jnp.bfloat16)
    return jnp.dot(hidden_bf, weights[2], preferred_element_type=jnp.float32)

def local_attention(query_block, key_block, value_block):
    query_count = query_block.shape[0]
    key_count = key_block.shape[0]
    query_heads = query_block.astype(jnp.float32).reshape(query_count, HEADS, HEAD_DIM)
    key_heads = key_block.astype(jnp.float32).reshape(key_count, HEADS, HEAD_DIM)
    value_heads = value_block.astype(jnp.float32).reshape(key_count, HEADS, HEAD_DIM)
    scores = jnp.einsum('qhe,khe->hqk', query_heads, key_heads) * HEAD_DIM ** (-0.5)
    weights_bf = jax.nn.softmax(scores, axis=-1).astype(jnp.bfloat16)
    mixed = jnp.einsum('hqk,khe->qhe', weights_bf.astype(jnp.float32), value_heads)
    return mixed.reshape(query_count, D)

def reference(key_tokens, value_tokens, queries, token_rate, fast_weights):
    block_count = TOKENS // TOK_DEV
    key_normed = rms_rows(key_tokens.astype(jnp.float32)).astype(jnp.bfloat16)
    signal = (-(token_rate[:, None] * value_tokens.astype(jnp.float32))).astype(jnp.bfloat16)

    def accumulate(running, pair):
        return (running + gradient_rows(fast_weights, pair[0], pair[1]), None)
    gradient, _ = lax.scan(accumulate, jnp.zeros((3, HID, D), jnp.float32), (key_normed.reshape(block_count, TOK_DEV, D), signal.reshape(block_count, TOK_DEV, D)))
    old_rows = fast_weights.astype(jnp.float32)
    stepped = old_rows - gradient
    updated = (stepped * jnp.sqrt(lax.optimization_barrier(jnp.mean(old_rows * old_rows, axis=-1, keepdims=True)) + epsilon) / jnp.sqrt(lax.optimization_barrier(jnp.mean(stepped * stepped, axis=-1, keepdims=True)) + epsilon)).astype(jnp.bfloat16)
    query_normed = rms_rows(queries.astype(jnp.float32)).astype(jnp.bfloat16)

    def per_block(group):
        query_block, key_block, value_block, normed_block = group
        total = fast_apply(updated, normed_block) + local_attention(query_block, key_block, value_block)
        return total.astype(jnp.bfloat16)
    result = lax.map(per_block, (queries.reshape(block_count, Q_DEV, D), key_tokens.reshape(block_count, TOK_DEV, D), value_tokens.reshape(block_count, TOK_DEV, D), query_normed.reshape(block_count, Q_DEV, D)))
    return result.reshape(QUERIES, D)
```

```python
import functools

import jax
import jax.numpy as jnp
from jax import lax
from jax.experimental import pallas as pl
from jax.experimental.pallas import tpu as pltpu
from jax.sharding import PartitionSpec as P

D = 768
TOK = 128
EPS = 1e-06
NX, NY, NZ = 4, 4, 8
ROWS = 6
BLK = NZ * ROWS
PACK = 48
MESH = pl.DeviceIdType.MESH
F32 = jnp.float32
BF16 = jnp.bfloat16


def dot_nt(a, b):
    return lax.dot_general(a, b, (((1,), (1,)), ((), ())), preferred_element_type=F32)


def dot_nn(a, b):
    return lax.dot_general(a, b, (((1,), (0,)), ((), ())), preferred_element_type=F32)


def device(x, y, z, c):
    return ((z // 4) * 2 + c, (z % 4) * 16 + y * 4 + x)


def rms_scale(rows):
    return lax.rsqrt(jnp.mean(rows * rows, axis=-1, keepdims=True) + EPS)


def kernel(
    key_ref, val_ref, qry_ref, rate_ref, w_ref, out_ref,
    wpk, az0, w, ks, qn, act, rys, ryr, rzs, rzr, az1, wu, unp, gu, hid_q, fo, ps, pr, att,
    s_az0, r_az0, s_wy, r_wy, s_tok, r_tok, s_tokc, r_tokc, s_q, r_q,
    s_ry, r_ry, s_rz, r_rz, s_az, r_az, s_ay, r_ay, s_ac, r_ac, s_p, r_p,
):
    g = lax.axis_index("grp")
    d = lax.axis_index("dev")
    x, y, z, c = d % 4, (d // 4) % 4, (g // 2) * 4 + d // 16, g % 2
    other = device(x, y, z, 1 - c)
    xs = [device((x + k) % NX, y, z, c) for k in range(NX)]
    ys = [device(x, (y + k) % NY, z, c) for k in range(NY)]
    zs = [device(x, y, (z + k) % NZ, c) for k in range(NZ)]

    barrier = pltpu.get_barrier_semaphore()
    peers = [other] + xs[1:] + ys[1:] + zs[1:]
    for peer in peers:
        pl.semaphore_signal(barrier, inc=1, device_id=peer, device_id_type=MESH)
    pl.semaphore_wait(barrier, len(peers))

    def send(src, dst, ssem, rsem, peer):
        pltpu.make_async_remote_copy(
            src_ref=src, dst_ref=dst, send_sem=ssem, recv_sem=rsem, device_id=peer, device_id_type=MESH
        ).start()

    def wait(ref, sem):
        pltpu.make_async_copy(ref, ref, sem).wait()

    wpk[...] = jnp.zeros_like(wpk)
    for m in range(3):
        rows = w_ref[m].astype(F32)
        for j in range(6):
            wpk[m, j * 8 : j * 8 + ROWS, :] = rows[:, j * 128 : (j + 1) * 128]
    az0[z] = wpk[...].astype(BF16)
    for k in range(1, NZ):
        send(az0.at[z], az0.at[z], s_az0, r_az0, zs[k])

    slot = x * 2 + c
    keys = key_ref[...].astype(F32)
    ks[0, slot] = (keys * rms_scale(keys)).astype(BF16)
    ks[1, slot] = (-(rate_ref[...] * val_ref[...].astype(F32))).astype(BF16)
    for k in (2, 1, 3):
        send(ks.at[:, slot], ks.at[:, slot], s_tok.at[k - 1], r_tok.at[k - 1], xs[k])
    send(ks.at[:, slot], ks.at[:, slot], s_tokc.at[0], r_tokc.at[0], other)
    queries = qry_ref[...].astype(F32)
    qn[x] = (queries * rms_scale(queries)).astype(BF16)

    def unpack(m, piece, store):
        for zz in range(NZ):
            unp[m, :, zz * ROWS : zz * ROWS + 8, :] = piece(zz).astype(F32).reshape(6, 8, 128)
        for j in range(6):
            store(j, unp[m, j, :BLK, :].astype(BF16))

    wait(az0.at[pl.ds(0, NZ - 1)], r_az0)
    for m in range(3):
        def put_old(j, v, m=m):
            w[m, y, :, j * 128 : (j + 1) * 128] = v
        unpack(m, lambda zz, m=m: az0[zz, m], put_old)
    for k in range(1, NY):
        send(w.at[:, y], w.at[:, y], s_wy, r_wy, ys[k])

    lane = lax.broadcasted_iota(jnp.int32, (TOK, 128), 1)
    for p in range(6):
        cols = slice(p * 128, (p + 1) * 128)
        qp, kp, vp = qry_ref[:, cols], key_ref[:, cols], val_ref[:, cols]
        zero = jnp.zeros_like(qp)
        both = jnp.concatenate([jnp.where(lane < 64, qp, zero), jnp.where(lane < 64, zero, qp)], axis=0)
        scores = dot_nt(both, kp) * 0.125
        e = jnp.exp(scores - jnp.max(scores, axis=-1, keepdims=True))
        probs = (e / jnp.sum(e, axis=-1, keepdims=True)).astype(BF16)
        mixed = dot_nn(probs, vp)
        att[:, cols] = jnp.where(lane < 64, mixed[:TOK], mixed[TOK:])

    def token_slot(k, core):
        return ((x + NX - k) % NX) * 2 + core
    for k in (1, 3, 2):
        sl = token_slot(k, c)
        wait(ks.at[:, sl], r_tok.at[k - 1])
        send(ks.at[:, sl], ks.at[:, sl], s_tokc.at[k], r_tokc.at[k], other)
    for k in (2, 1, 3):
        send(qn.at[x], qn.at[x], s_q, r_q, xs[k])

    wait(w.at[:, pl.ds(0, NY - 1)], r_wy)
    w1 = w[0].reshape(NY * BLK, D)
    w3 = w[1].reshape(NY * BLK, D)
    w2 = w[2].reshape(NY * BLK, D)
    for k in (0, 1, 3, 2):
        sl = token_slot(k, 1 - c)
        wait(ks.at[:, sl], r_tokc.at[k])
        xx = (x + NX - k) % NX
        kn = ks[0, pl.ds(xx * 2, 2)].reshape(2 * TOK, D)
        sg = ks[1, pl.ds(xx * 2, 2)].reshape(2 * TOK, D)
        gate = dot_nt(w1, kn)
        up = dot_nt(w3, kn)
        hgrad = dot_nt(w2, sg)
        sig = jax.nn.sigmoid(gate)
        silu = gate * sig
        act[2, xx] = (silu * up).astype(BF16)
        act[0, xx] = (hgrad * up * sig * (1.0 + gate * (1.0 - sig))).astype(BF16)
        act[1, xx] = (hgrad * silu).astype(BF16)

    order = (2, 0, 1)
    for m in order:
        src = 1 if m == 2 else 0
        total = None
        for xx in range(NX):
            term = dot_nn(act[m, xx], ks[src, 2 * xx : 2 * xx + 2].reshape(2 * TOK, D))
            total = term if total is None else total + term
        rys[m] = total.astype(BF16).reshape(NY, BLK, D)
        for k in (2, 1, 3):
            send(rys.at[m, (y + k) % NY], ryr.at[m, k - 1], s_ry, r_ry.at[m], ys[k])

    unp[:, :, BLK:, :] = jnp.zeros((3, 6, 8, 128), F32)
    for m in order:
        wait(ryr.at[m], r_ry.at[m])
        total = rys[m, y].astype(F32)
        for k in range(NY - 1):
            total = total + ryr[m, k].astype(F32)
        for j in range(6):
            unp[m, j, :BLK, :] = total[:, j * 128 : (j + 1) * 128]
        for zz in range(NZ):
            rzs[m, zz] = unp[m, :, zz * ROWS : zz * ROWS + 8, :].reshape(PACK, 128).astype(BF16)
        for k in (4, 3, 5, 2, 6, 1, 7):
            send(rzs.at[m, (z + k) % NZ], rzr.at[m, k - 1], s_rz, r_rz.at[m], zs[k])

    for m in order:
        wait(rzr.at[m], r_rz.at[m])
        grad = rzs[m, z].astype(F32)
        for k in range(NZ - 1):
            grad = grad + rzr[m, k].astype(F32)
        old = wpk[m].reshape(6, 8, 128)
        stepped = old - grad.reshape(6, 8, 128)
        old_ms = jnp.sum(jnp.sum(old * old, axis=0), axis=-1, keepdims=True) * (1.0 / D)
        new_ms = jnp.sum(jnp.sum(stepped * stepped, axis=0), axis=-1, keepdims=True) * (1.0 / D)
        upd = stepped * jnp.sqrt(old_ms + EPS)[None] / jnp.sqrt(new_ms + EPS)[None]
        az1[m, z] = upd.reshape(PACK, 128).astype(BF16)
        for k in (4, 3, 5, 2, 6, 1, 7):
            send(az1.at[m, z], az1.at[m, z], s_az, r_az.at[m], zs[k])

    for m in order:
        wait(az1.at[m, pl.ds(0, NZ - 1)], r_az.at[m])
        def put_new(j, v, m=m):
            wu[m, c, y, :, j * 128 : (j + 1) * 128] = v
        unpack(m, lambda zz, m=m: az1[m, zz], put_new)
        for k in (2, 1, 3):
            send(wu.at[m, c, y], wu.at[m, c, y], s_ay, r_ay.at[m], ys[k])

    for m in order:
        wait(wu.at[m, c, pl.ds(0, NY - 1)], r_ay.at[m])
        send(wu.at[m, c], wu.at[m, c], s_ac, r_ac.at[m], other)

    wait(qn.at[pl.ds(0, NX - 1)], r_q)
    hid = 2 * NY * BLK
    for m in (0, 1):
        wait(wu.at[m, 1 - c], r_ac.at[m])
        gu[m] = dot_nt(qn[...].reshape(NX * TOK, D), wu[m].reshape(hid, D))
    gate = gu[0]
    hid_q[...] = (gate * jax.nn.sigmoid(gate) * gu[1]).astype(BF16)
    wait(wu.at[2, 1 - c], r_ac.at[2])
    part = dot_nn(hid_q[...], wu[2].reshape(hid, D)).reshape(NX, TOK, D)
    fo[...] = part
    ps[...] = part.astype(BF16)
    for k in (2, 1, 3):
        send(ps.at[(x + k) % NX], pr.at[k - 1], s_p, r_p, xs[k])

    wait(az0.at[pl.ds(0, NZ - 1)], s_az0)
    for k in range(NX - 1):
        wait(ks.at[:, 0], s_tok.at[k])
    for k in range(NX):
        wait(ks.at[:, 0], s_tokc.at[k])
    wait(w.at[:, pl.ds(0, NY - 1)], s_wy)
    wait(qn.at[pl.ds(0, NX - 1)], s_q)
    wait(ryr, s_ry)
    wait(rzr, s_rz)
    wait(az1.at[:, pl.ds(0, NZ - 1)], s_az)
    wait(wu.at[:, 0, pl.ds(0, NY - 1)], s_ay)
    wait(wu.at[:, 0], s_ac)
    wait(pr, s_p)

    wait(pr, r_p)
    result = fo[x] + att[...]
    for k in range(NX - 1):
        result = result + pr[k].astype(F32)
    out_ref[...] = result.astype(BF16)


def body(key_tokens, value_tokens, queries, token_rate, fast_weights):
    vmem = pl.BlockSpec(memory_space=pltpu.VMEM)
    dma = pltpu.SemaphoreType.DMA
    return pl.pallas_call(
        kernel,
        name="ttt_layer",
        out_shape=jax.ShapeDtypeStruct((TOK, D), BF16),
        in_specs=[vmem] * 5,
        out_specs=vmem,
        scratch_shapes=[
            pltpu.VMEM((3, PACK, 128), F32),
            pltpu.VMEM((NZ, 3, PACK, 128), BF16),
            pltpu.VMEM((3, NY, BLK, D), BF16),
            pltpu.VMEM((2, 2 * NX, TOK, D), BF16),
            pltpu.VMEM((NX, TOK, D), BF16),
            pltpu.VMEM((3, NX, NY * BLK, 2 * TOK), BF16),
            pltpu.VMEM((3, NY, BLK, D), BF16),
            pltpu.VMEM((3, NY - 1, BLK, D), BF16),
            pltpu.VMEM((3, NZ, PACK, 128), BF16),
            pltpu.VMEM((3, NZ - 1, PACK, 128), BF16),
            pltpu.VMEM((3, NZ, PACK, 128), BF16),
            pltpu.VMEM((3, 2, NY, BLK, D), BF16),
            pltpu.VMEM((3, 6, BLK + 8, 128), F32),
            pltpu.VMEM((2, NX * TOK, 2 * NY * BLK), F32),
            pltpu.VMEM((NX * TOK, 2 * NY * BLK), BF16),
            pltpu.VMEM((NX, TOK, D), F32),
            pltpu.VMEM((NX, TOK, D), BF16),
            pltpu.VMEM((NX - 1, TOK, D), BF16),
            pltpu.VMEM((TOK, D), F32),
            dma, dma, dma, dma,
            dma((NX - 1,)), dma((NX - 1,)), dma((NX,)), dma((NX,)), dma, dma,
            dma, dma((3,)), dma, dma((3,)), dma, dma((3,)), dma, dma((3,)), dma, dma((3,)),
            dma, dma,
        ],
        compiler_params=pltpu.CompilerParams(
            collective_id=0, has_side_effects=True, vmem_limit_bytes=48 << 20
        ),
    )(key_tokens, value_tokens, queries, token_rate.reshape(TOK, 1), fast_weights)


def solution(mesh):
    rows = P(("grp", "dev"), None)
    in_specs = (rows, rows, rows, P(("grp", "dev")), P(None, ("grp", "dev"), None))
    return jax.shard_map(body, mesh=mesh, in_specs=in_specs, out_specs=rows, check_vma=False)
```

```python
import functools

import jax
import jax.numpy as jnp
from jax import lax
from jax.experimental import pallas as pl
from jax.experimental.pallas import tpu as pltpu
from jax.sharding import PartitionSpec as P

D = 768
TOK = 128
EPS = 1e-06
NX, NY, NZ = 4, 4, 8
ROWS = 6
BLK = NZ * ROWS
PACK = 48
MESH = pl.DeviceIdType.MESH
F32 = jnp.float32
BF16 = jnp.bfloat16


def dot_nt(a, b):
    return lax.dot_general(a, b, (((1,), (1,)), ((), ())), preferred_element_type=F32)


def dot_nn(a, b):
    return lax.dot_general(a, b, (((1,), (0,)), ((), ())), preferred_element_type=F32)


def device(x, y, z, c):
    return ((z // 4) * 2 + c, (z % 4) * 16 + y * 4 + x)


def rms_scale(rows):
    return lax.rsqrt(jnp.mean(rows * rows, axis=-1, keepdims=True) + EPS)


def kernel(
    key_hbm, val_hbm, qry_hbm, rate_hbm, w_hbm, out_ref,
    key_ref, val_ref, qry_ref, rate_ref, w_ref,
    wpk, az0, w, ks, qn, gs, act, rys, ryr, rzs, rzr, az1, wu, unp, gu, hid_q, ps, pr, att,
    s_in, s_az0, r_az0, s_wy, r_wy, s_tok, r_tok, r_tokc, s_q, r_q,
    s_ry, r_ry, s_rz, r_rz, s_az, r_az, s_ay, r_ay, s_ac, r_ac, s_p, r_p,
):
    g = lax.axis_index("grp")
    d = lax.axis_index("dev")
    x, y, z, c = d % 4, (d // 4) % 4, (g // 2) * 4 + d // 16, g % 2
    other = device(x, y, z, 1 - c)
    xs = [device((x + k) % NX, y, z, c) for k in range(NX)]
    ys = [device(x, (y + k) % NY, z, c) for k in range(NY)]
    zs = [device(x, y, (z + k) % NZ, c) for k in range(NZ)]
    far_first_z = (4, 3, 5, 2, 6, 1, 7)

    barrier = pltpu.get_barrier_semaphore()
    peers = [other] + xs[1:] + ys[1:] + zs[1:]
    for peer in peers:
        pl.semaphore_signal(barrier, inc=1, device_id=peer, device_id_type=MESH)

    fetches = [
        pltpu.make_async_copy(src, dst, s_in.at[i])
        for i, (src, dst) in enumerate(
            [(w_hbm, w_ref), (key_hbm, key_ref), (val_hbm, val_ref), (rate_hbm, rate_ref), (qry_hbm, qry_ref)]
        )
    ]
    for fetch in fetches:
        fetch.start()

    def send(src, dst, ssem, rsem, peer):
        pltpu.make_async_remote_copy(
            src_ref=src, dst_ref=dst, send_sem=ssem, recv_sem=rsem, device_id=peer, device_id_type=MESH
        ).start()

    def wait(ref, sem):
        pltpu.make_async_copy(ref, ref, sem).wait()

    wpk[...] = jnp.zeros_like(wpk)
    fetches[0].wait()
    for m in range(3):
        rows = w_ref[m].astype(F32)
        for j in range(6):
            wpk[m, j * 8 : j * 8 + ROWS, :] = rows[:, j * 128 : (j + 1) * 128]
        az0[m, z] = wpk[m].astype(BF16)

    slot = x * 2 + c
    fetches[1].wait()
    keys = key_ref[...].astype(F32)
    ks[0, slot] = (keys * rms_scale(keys)).astype(BF16)
    fetches[2].wait()
    fetches[3].wait()
    diagonal = lax.broadcasted_iota(jnp.int32, (TOK, TOK), 0) == lax.broadcasted_iota(jnp.int32, (TOK, TOK), 1)
    rate = jnp.sum(jnp.where(diagonal, rate_ref[...], 0.0), axis=-1, keepdims=True)
    ks[1, slot] = (-(rate * val_ref[...].astype(F32))).astype(BF16)

    pl.semaphore_wait(barrier, len(peers))

    def send_tok(kind, sl, sem, peer):
        send(ks.at[kind, sl], ks.at[kind, sl], s_tok, sem, peer)
    for k in far_first_z:
        send(az0.at[0, z], az0.at[0, z], s_az0, r_az0.at[0], zs[k])
    send_tok(0, slot, r_tok.at[0, 0], xs[1])
    send_tok(1, slot, r_tok.at[2, 1], xs[3])
    send_tok(1, slot, r_tok.at[0, 1], xs[1])
    send_tok(0, slot, r_tok.at[2, 0], xs[3])
    for kind in range(2):
        send_tok(kind, slot, r_tokc.at[0, kind], other)
    for m in (1, 2):
        for k in far_first_z:
            send(az0.at[m, z], az0.at[m, z], s_az0, r_az0.at[m], zs[k])
    fetches[4].wait()
    queries = qry_ref[...].astype(F32)
    qn[x] = (queries * rms_scale(queries)).astype(BF16)

    def token_slot(k, core):
        return ((x + NX - k) % NX) * 2 + core

    def tokens_in(k, kind, onward):
        sl = token_slot(k, c)
        wait(ks.at[kind, sl], r_tok.at[k - 1, kind])
        if onward is not None:
            send_tok(kind, sl, r_tok.at[1, kind], onward)
        send_tok(kind, sl, r_tokc.at[k, kind], other)

    def unpack(m, packed, store):
        for zz in range(NZ):
            unp[m, :, zz * ROWS : zz * ROWS + 8, :] = packed[m, zz].astype(F32).reshape(6, 8, 128)
        for j in range(6):
            store(j, unp[m, j, :BLK, :].astype(BF16))

    def old_weights(m):
        wait(az0.at[m, pl.ds(0, NZ - 1)], r_az0.at[m])
        def put(j, v):
            w[m, y, :, j * 128 : (j + 1) * 128] = v
        unpack(m, az0, put)
        for k in (2, 1, 3):
            send(w.at[m, y], w.at[m, y], s_wy, r_wy.at[m], ys[k])

    old_weights(0)
    old_weights(1)
    tokens_in(1, 0, xs[1])
    tokens_in(3, 1, xs[3])
    old_weights(2)

    lane = lax.broadcasted_iota(jnp.int32, (TOK, 128), 1)
    for p in range(6):
        cols = slice(p * 128, (p + 1) * 128)
        qp, kp, vp = qry_ref[:, cols], key_ref[:, cols], val_ref[:, cols]
        zero = jnp.zeros_like(qp)
        both = jnp.concatenate([jnp.where(lane < 64, qp, zero), jnp.where(lane < 64, zero, qp)], axis=0)
        scores = dot_nt(both, kp) * 0.125
        e = jnp.exp(scores - jnp.max(scores, axis=-1, keepdims=True))
        probs = (e / jnp.sum(e, axis=-1, keepdims=True)).astype(BF16)
        mixed = dot_nn(probs, vp)
        att[:, cols] = jnp.where(lane < 64, mixed[:TOK], mixed[TOK:])

    tokens_in(1, 1, None)
    tokens_in(3, 0, None)

    def chunk(kind, k):
        xx = (x + NX - k) % NX
        return ks[kind, pl.ds(xx * 2, 2)].reshape(2 * TOK, D)

    def forward(k):
        wait(ks.at[0, 0], r_tokc.at[k, 0])
        kn = chunk(0, k)
        gate = dot_nt(w[0].reshape(NY * BLK, D), kn)
        up = dot_nt(w[1].reshape(NY * BLK, D), kn)
        gs[0, k] = gate
        gs[1, k] = up
        act[2, k] = (gate * jax.nn.sigmoid(gate) * up).astype(BF16)

    def backward(k):
        hgrad = dot_nt(w[2].reshape(NY * BLK, D), chunk(1, k))
        gate, up = gs[0, k], gs[1, k]
        sig = jax.nn.sigmoid(gate)
        act[0, k] = (hgrad * up * sig * (1.0 + gate * (1.0 - sig))).astype(BF16)
        act[1, k] = (hgrad * (gate * sig)).astype(BF16)

    wait(w.at[0, pl.ds(0, NY - 1)], r_wy.at[0])
    wait(w.at[1, pl.ds(0, NY - 1)], r_wy.at[1])
    for k in (0, 1, 3):
        forward(k)
    tokens_in(2, 0, None)
    tokens_in(2, 1, None)
    for k in (2, 1, 3):
        send(qn.at[x], qn.at[x], s_q, r_q, xs[k])
    forward(2)
    for k in (0, 1, 3, 2):
        wait(ks.at[1, 0], r_tokc.at[k, 1])

    def gradient(m):
        total = None
        for k in range(NX):
            term = dot_nn(act[m, k], chunk(1 if m == 2 else 0, k))
            total = term if total is None else total + term
        rys[m] = total.astype(BF16).reshape(NY, BLK, D)
        for k in (2, 1, 3):
            send(rys.at[m, (y + k) % NY], ryr.at[m, k - 1], s_ry, r_ry.at[m], ys[k])

    gradient(2)
    wait(w.at[2, pl.ds(0, NY - 1)], r_wy.at[2])
    for k in (0, 1, 3, 2):
        backward(k)
    gradient(0)
    gradient(1)

    order = (2, 0, 1)
    unp[:, :, BLK:, :] = jnp.zeros((3, 6, 8, 128), F32)
    for m in order:
        wait(ryr.at[m], r_ry.at[m])
        total = rys[m, y].astype(F32)
        for k in range(NY - 1):
            total = total + ryr[m, k].astype(F32)
        for j in range(6):
            unp[m, j, :BLK, :] = total[:, j * 128 : (j + 1) * 128]
        for zz in range(NZ):
            rzs[m, zz] = unp[m, :, zz * ROWS : zz * ROWS + 8, :].reshape(PACK, 128).astype(BF16)
        for k in far_first_z:
            send(rzs.at[m, (z + k) % NZ], rzr.at[m, k - 1], s_rz, r_rz.at[m], zs[k])

    for m in order:
        wait(rzr.at[m], r_rz.at[m])
        grad = rzs[m, z].astype(F32)
        for k in range(NZ - 1):
            grad = grad + rzr[m, k].astype(F32)
        old = wpk[m].reshape(6, 8, 128)
        stepped = old - grad.reshape(6, 8, 128)
        old_ms = jnp.sum(jnp.sum(old * old, axis=0), axis=-1, keepdims=True) * (1.0 / D)
        new_ms = jnp.sum(jnp.sum(stepped * stepped, axis=0), axis=-1, keepdims=True) * (1.0 / D)
        upd = stepped * jnp.sqrt(old_ms + EPS)[None] / jnp.sqrt(new_ms + EPS)[None]
        az1[m, z] = upd.reshape(PACK, 128).astype(BF16)
        for k in far_first_z:
            send(az1.at[m, z], az1.at[m, z], s_az, r_az.at[m], zs[k])

    for m in order:
        wait(az1.at[m, pl.ds(0, NZ - 1)], r_az.at[m])
        def put_new(j, v, m=m):
            wu[m, c, y, :, j * 128 : (j + 1) * 128] = v
        unpack(m, az1, put_new)
        for k in (2, 1, 3):
            send(wu.at[m, c, y], wu.at[m, c, y], s_ay, r_ay.at[m], ys[k])

    wait(qn.at[pl.ds(0, NX - 1)], r_q)
    for m in order:
        wait(wu.at[m, c, pl.ds(0, NY - 1)], r_ay.at[m])
        send(wu.at[m, c], wu.at[m, c], s_ac, r_ac.at[m], other)
        if m < 2:
            gu[m, 0] = dot_nt(qn[...].reshape(NX * TOK, D), wu[m, c].reshape(NY * BLK, D))

    def query_hidden(half):
        gate = gu[0, half]
        hid_q[half] = (gate * jax.nn.sigmoid(gate) * gu[1, half]).astype(BF16).reshape(NX, TOK, NY * BLK)

    query_hidden(0)
    for m in (0, 1):
        wait(wu.at[m, 1 - c], r_ac.at[m])
        gu[m, 1] = dot_nt(qn[...].reshape(NX * TOK, D), wu[m, 1 - c].reshape(NY * BLK, D))
    query_hidden(1)
    wait(wu.at[2, 1 - c], r_ac.at[2])
    down_own = wu[2, c].reshape(NY * BLK, D)
    down_other = wu[2, 1 - c].reshape(NY * BLK, D)
    for k in (2, 1, 3, 0):
        to = (x + k) % NX
        part = dot_nn(hid_q[0, to], down_own) + dot_nn(hid_q[1, to], down_other)
        if k:
            ps[k - 1] = part.astype(BF16)
            send(ps.at[k - 1], pr.at[k - 1], s_p, r_p, xs[k])
        else:
            att[...] += part

    wait(az0.at[:, pl.ds(0, NZ - 1)], s_az0)
    for _ in range(7):
        wait(ks.at[:, 0], s_tok)
    wait(w.at[:, pl.ds(0, NY - 1)], s_wy)
    wait(qn.at[pl.ds(0, NX - 1)], s_q)
    wait(ryr, s_ry)
    wait(rzr, s_rz)
    wait(az1.at[:, pl.ds(0, NZ - 1)], s_az)
    wait(wu.at[:, 0, pl.ds(0, NY - 1)], s_ay)
    wait(wu.at[:, 0], s_ac)
    wait(pr, s_p)

    wait(pr, r_p)
    result = att[...]
    for k in range(NX - 1):
        result = result + pr[k].astype(F32)
    out_ref[...] = result.astype(BF16)


def body(key_tokens, value_tokens, queries, token_rate, fast_weights):
    vmem = pltpu.VMEM
    dma = pltpu.SemaphoreType.DMA
    return pl.pallas_call(
        kernel,
        name="ttt_layer",
        out_shape=jax.ShapeDtypeStruct((TOK, D), BF16),
        in_specs=[pl.BlockSpec(memory_space=pl.ANY)] * 5,
        out_specs=pl.BlockSpec(memory_space=pltpu.VMEM),
        scratch_shapes=[
            vmem((TOK, D), BF16),
            vmem((TOK, D), BF16),
            vmem((TOK, D), BF16),
            vmem((1, TOK), F32),
            vmem((3, ROWS, D), BF16),
            vmem((3, PACK, 128), F32),
            vmem((3, NZ, PACK, 128), BF16),
            vmem((3, NY, BLK, D), BF16),
            vmem((2, 2 * NX, TOK, D), BF16),
            vmem((NX, TOK, D), BF16),
            vmem((2, NX, NY * BLK, 2 * TOK), F32),
            vmem((3, NX, NY * BLK, 2 * TOK), BF16),
            vmem((3, NY, BLK, D), BF16),
            vmem((3, NY - 1, BLK, D), BF16),
            vmem((3, NZ, PACK, 128), BF16),
            vmem((3, NZ - 1, PACK, 128), BF16),
            vmem((3, NZ, PACK, 128), BF16),
            vmem((3, 2, NY, BLK, D), BF16),
            vmem((3, 6, BLK + 8, 128), F32),
            vmem((2, 2, NX * TOK, NY * BLK), F32),
            vmem((2, NX, TOK, NY * BLK), BF16),
            vmem((NX - 1, TOK, D), BF16),
            vmem((NX - 1, TOK, D), BF16),
            vmem((TOK, D), F32),
            dma((5,)), dma, dma((3,)), dma, dma((3,)), dma, dma((3, 2)), dma((NX, 2)), dma, dma,
            dma, dma((3,)), dma, dma((3,)), dma, dma((3,)), dma, dma((3,)), dma, dma((3,)),
            dma, dma,
        ],
        compiler_params=pltpu.CompilerParams(
            collective_id=0, has_side_effects=True, vmem_limit_bytes=56 << 20
        ),
    )(key_tokens, value_tokens, queries, token_rate.reshape(1, TOK), fast_weights)


def solution(mesh):
    rows = P(("grp", "dev"), None)
    in_specs = (rows, rows, rows, P(("grp", "dev")), P(None, ("grp", "dev"), None))
    return jax.shard_map(body, mesh=mesh, in_specs=in_specs, out_specs=rows, check_vma=False)
```

```python
import functools

import jax
import jax.numpy as jnp
from jax import lax
from jax.experimental import pallas as pl
from jax.experimental.pallas import tpu as pltpu
from jax.sharding import PartitionSpec as P

D = 768
TOK = 128
EPS = 1e-06
NX, NY, NZ = 4, 4, 8
ROWS = 6
BLK = NZ * ROWS
PACK = 48
MESH = pl.DeviceIdType.MESH
F32 = jnp.float32
BF16 = jnp.bfloat16


def dot_nt(a, b):
    return lax.dot_general(a, b, (((1,), (1,)), ((), ())), preferred_element_type=F32)


def dot_nn(a, b):
    return lax.dot_general(a, b, (((1,), (0,)), ((), ())), preferred_element_type=F32)


def device(x, y, z, c):
    return ((z // 4) * 2 + c, (z % 4) * 16 + y * 4 + x)


def rms_scale(rows):
    return lax.rsqrt(jnp.mean(rows * rows, axis=-1, keepdims=True) + EPS)


def kernel(
    key_hbm, val_hbm, qry_hbm, rate_hbm, w_hbm, out_ref,
    key_ref, val_ref, qry_ref, rate_ref, w_ref,
    wpk, az0, w, ks, qn, gs, act, rys, ryr, rzs, rzr, az1, wu, unp, gu, hid_q, ps, pr, att,
    s_in, s_az0, r_az0, s_wy, r_wy, s_tok, r_tok, r_tokc, s_q, r_q,
    s_ry, r_ry, s_rz, r_rz, s_az, r_az, s_ay, r_ay, s_ac, r_ac, s_p, r_p,
):
    g = lax.axis_index("grp")
    d = lax.axis_index("dev")
    x, y, z, c = d % 4, (d // 4) % 4, (g // 2) * 4 + d // 16, g % 2
    other = device(x, y, z, 1 - c)
    xs = [device((x + k) % NX, y, z, c) for k in range(NX)]
    ys = [device(x, (y + k) % NY, z, c) for k in range(NY)]
    zs = [device(x, y, (z + k) % NZ, c) for k in range(NZ)]
    pos = (y * (1 - c) + x * c, x * (1 - c) + y * c)
    lines = (
        [device((x + k * c) % NX, (y + k * (1 - c)) % NY, z, c) for k in range(NX)],
        [device((x + k * (1 - c)) % NX, (y + k * c) % NY, z, c) for k in range(NX)],
    )
    far_first_z = (4, 3, 5, 2, 6, 1, 7)

    barrier = pltpu.get_barrier_semaphore()
    peers = [other] + xs[1:] + ys[1:] + zs[1:]
    for peer in peers:
        pl.semaphore_signal(barrier, inc=1, device_id=peer, device_id_type=MESH)

    fetches = [
        pltpu.make_async_copy(src, dst, s_in.at[i])
        for i, (src, dst) in enumerate(
            [(w_hbm, w_ref), (key_hbm, key_ref), (val_hbm, val_ref), (rate_hbm, rate_ref), (qry_hbm, qry_ref)]
        )
    ]
    for fetch in fetches:
        fetch.start()

    def send(src, dst, ssem, rsem, peer):
        pltpu.make_async_remote_copy(
            src_ref=src, dst_ref=dst, send_sem=ssem, recv_sem=rsem, device_id=peer, device_id_type=MESH
        ).start()

    def wait(ref, sem):
        pltpu.make_async_copy(ref, ref, sem).wait()

    wpk[...] = jnp.zeros_like(wpk)
    fetches[0].wait()
    for m in range(3):
        rows = w_ref[m].astype(F32)
        for j in range(6):
            wpk[m, j * 8 : j * 8 + ROWS, :] = rows[:, j * 128 : (j + 1) * 128]
        az0[m, z] = wpk[m].astype(BF16)

    slot = x * 2 + c
    fetches[1].wait()
    keys = key_ref[...].astype(F32)
    ks[0, slot] = (keys * rms_scale(keys)).astype(BF16)
    fetches[2].wait()
    fetches[3].wait()
    diagonal = lax.broadcasted_iota(jnp.int32, (TOK, TOK), 0) == lax.broadcasted_iota(jnp.int32, (TOK, TOK), 1)
    rate = jnp.sum(jnp.where(diagonal, rate_ref[...], 0.0), axis=-1, keepdims=True)
    ks[1, slot] = (-(rate * val_ref[...].astype(F32))).astype(BF16)

    pl.semaphore_wait(barrier, len(peers))

    def send_tok(kind, sl, sem, peer):
        send(ks.at[kind, sl], ks.at[kind, sl], s_tok, sem, peer)
    for k in far_first_z:
        send(az0.at[0, z], az0.at[0, z], s_az0, r_az0.at[0], zs[k])
    send_tok(0, slot, r_tok.at[0, 0], xs[1])
    send_tok(1, slot, r_tok.at[2, 1], xs[3])
    send_tok(1, slot, r_tok.at[0, 1], xs[1])
    send_tok(0, slot, r_tok.at[2, 0], xs[3])
    for kind in range(2):
        send_tok(kind, slot, r_tokc.at[0, kind], other)
    for m in (1, 2):
        for k in far_first_z:
            send(az0.at[m, z], az0.at[m, z], s_az0, r_az0.at[m], zs[k])
    fetches[4].wait()
    queries = qry_ref[...].astype(F32)
    normed = (queries * rms_scale(queries)).astype(BF16)
    qn[0, x] = normed
    qn[1, y] = normed

    def token_slot(k, core):
        return ((x + NX - k) % NX) * 2 + core

    def tokens_in(k, kind, onward):
        sl = token_slot(k, c)
        wait(ks.at[kind, sl], r_tok.at[k - 1, kind])
        if onward is not None:
            send_tok(kind, sl, r_tok.at[1, kind], onward)
        send_tok(kind, sl, r_tokc.at[k, kind], other)

    def unpack(m, packed, store):
        for zz in range(NZ):
            unp[m, :, zz * ROWS : zz * ROWS + 8, :] = packed[m, zz].astype(F32).reshape(6, 8, 128)
        for j in range(6):
            store(j, unp[m, j, :BLK, :].astype(BF16))

    def old_weights(m):
        wait(az0.at[m, pl.ds(0, NZ - 1)], r_az0.at[m])
        def put(j, v):
            w[m, y, :, j * 128 : (j + 1) * 128] = v
        unpack(m, az0, put)
        for k in (2, 1, 3):
            send(w.at[m, y], w.at[m, y], s_wy, r_wy.at[m], ys[k])

    old_weights(0)
    old_weights(1)
    tokens_in(1, 0, xs[1])
    tokens_in(3, 1, xs[3])
    old_weights(2)

    lane = lax.broadcasted_iota(jnp.int32, (TOK, 128), 1)
    for p in range(6):
        cols = slice(p * 128, (p + 1) * 128)
        qp, kp, vp = qry_ref[:, cols], key_ref[:, cols], val_ref[:, cols]
        zero = jnp.zeros_like(qp)
        both = jnp.concatenate([jnp.where(lane < 64, qp, zero), jnp.where(lane < 64, zero, qp)], axis=0)
        scores = dot_nt(both, kp) * 0.125
        e = jnp.exp(scores - jnp.max(scores, axis=-1, keepdims=True))
        probs = (e / jnp.sum(e, axis=-1, keepdims=True)).astype(BF16)
        mixed = dot_nn(probs, vp)
        att[:, cols] = jnp.where(lane < 64, mixed[:TOK], mixed[TOK:])

    tokens_in(1, 1, None)
    tokens_in(3, 0, None)

    def chunk(kind, k):
        xx = (x + NX - k) % NX
        return ks[kind, pl.ds(xx * 2, 2)].reshape(2 * TOK, D)

    def forward(k):
        wait(ks.at[0, 0], r_tokc.at[k, 0])
        kn = chunk(0, k)
        gate = dot_nt(w[0].reshape(NY * BLK, D), kn)
        up = dot_nt(w[1].reshape(NY * BLK, D), kn)
        gs[0, k] = gate
        gs[1, k] = up
        act[2, k] = (gate * jax.nn.sigmoid(gate) * up).astype(BF16)

    def backward(k):
        hgrad = dot_nt(w[2].reshape(NY * BLK, D), chunk(1, k))
        gate, up = gs[0, k], gs[1, k]
        sig = jax.nn.sigmoid(gate)
        act[0, k] = (hgrad * up * sig * (1.0 + gate * (1.0 - sig))).astype(BF16)
        act[1, k] = (hgrad * (gate * sig)).astype(BF16)

    wait(w.at[0, pl.ds(0, NY - 1)], r_wy.at[0])
    wait(w.at[1, pl.ds(0, NY - 1)], r_wy.at[1])
    for k in (0, 1, 3):
        forward(k)
    tokens_in(2, 0, None)
    tokens_in(2, 1, None)
    for k in (2, 1, 3):
        send(qn.at[0, x], qn.at[0, x], s_q, r_q.at[0], xs[k])
    forward(2)
    for k in (0, 1, 3, 2):
        wait(ks.at[1, 0], r_tokc.at[k, 1])

    def gradient(m):
        total = None
        for k in range(NX):
            term = dot_nn(act[m, k], chunk(1 if m == 2 else 0, k))
            total = term if total is None else total + term
        rys[m] = total.astype(BF16).reshape(NY, BLK, D)
        for k in (2, 1, 3):
            send(rys.at[m, (y + k) % NY], ryr.at[m, k - 1], s_ry, r_ry.at[m], ys[k])

    gradient(2)
    wait(w.at[2, pl.ds(0, NY - 1)], r_wy.at[2])
    for k in (0, 1, 3, 2):
        backward(k)
    gradient(0)
    gradient(1)
    for k in (2, 1, 3):
        send(qn.at[1, y], qn.at[1, y], s_q, r_q.at[1], ys[k])

    order = (2, 0, 1)
    unp[:, :, BLK:, :] = jnp.zeros((3, 6, 8, 128), F32)
    for m in order:
        wait(ryr.at[m], r_ry.at[m])
        total = rys[m, y].astype(F32)
        for k in range(NY - 1):
            total = total + ryr[m, k].astype(F32)
        for j in range(6):
            unp[m, j, :BLK, :] = total[:, j * 128 : (j + 1) * 128]
        for zz in range(NZ):
            rzs[m, zz] = unp[m, :, zz * ROWS : zz * ROWS + 8, :].reshape(PACK, 128).astype(BF16)
        for k in far_first_z:
            send(rzs.at[m, (z + k) % NZ], rzr.at[m, k - 1], s_rz, r_rz.at[m], zs[k])

    for m in order:
        wait(rzr.at[m], r_rz.at[m])
        grad = rzs[m, z].astype(F32)
        for k in range(NZ - 1):
            grad = grad + rzr[m, k].astype(F32)
        old = wpk[m].reshape(6, 8, 128)
        stepped = old - grad.reshape(6, 8, 128)
        old_ms = jnp.sum(jnp.sum(old * old, axis=0), axis=-1, keepdims=True) * (1.0 / D)
        new_ms = jnp.sum(jnp.sum(stepped * stepped, axis=0), axis=-1, keepdims=True) * (1.0 / D)
        upd = stepped * jnp.sqrt(old_ms + EPS)[None] / jnp.sqrt(new_ms + EPS)[None]
        az1[m, z] = upd.reshape(PACK, 128).astype(BF16)
        for k in far_first_z:
            send(az1.at[m, z], az1.at[m, z], s_az, r_az.at[m], zs[k])

    for m in order:
        wait(az1.at[m, pl.ds(0, NZ - 1)], r_az.at[m])
        def put_new(j, v, m=m):
            wu[m, c, pos[0], :, j * 128 : (j + 1) * 128] = v
        unpack(m, az1, put_new)
        for k in (2, 1, 3):
            send(wu.at[m, c, pos[0]], wu.at[m, c, pos[0]], s_ay, r_ay.at[m], lines[0][k])

    def project(m, half, core):
        gu[m, half] = dot_nt(qn[core].reshape(NX * TOK, D), wu[m, core].reshape(NY * BLK, D))

    def query_hidden(half):
        gate = gu[0, half]
        hid_q[half] = (gate * jax.nn.sigmoid(gate) * gu[1, half]).astype(BF16).reshape(NX, TOK, NY * BLK)

    def partial_outputs(half, core):
        down = wu[2, core].reshape(NY * BLK, D)
        for k in (2, 1, 3, 0):
            part = dot_nn(hid_q[half, (pos[1 - half] + k) % NX], down)
            if k:
                ps[half, k - 1] = part.astype(BF16)
                send(ps.at[half, k - 1], pr.at[half, k - 1], s_p, r_p.at[half], lines[1 - half][k])
            else:
                att[...] += part

    for axis in range(2):
        wait(qn.at[axis, pl.ds(0, NX - 1)], r_q.at[axis])
    for m in order:
        wait(wu.at[m, c, pl.ds(0, NY - 1)], r_ay.at[m])
        send(wu.at[m, c], wu.at[m, c], s_ac, r_ac.at[m], other)
        if m < 2:
            project(m, 0, c)
    query_hidden(0)
    partial_outputs(0, c)
    for m in (0, 1):
        wait(wu.at[m, 1 - c], r_ac.at[m])
        project(m, 1, 1 - c)
    query_hidden(1)
    wait(wu.at[2, 1 - c], r_ac.at[2])
    partial_outputs(1, 1 - c)

    wait(az0.at[:, pl.ds(0, NZ - 1)], s_az0)
    for _ in range(7):
        wait(ks.at[:, 0], s_tok)
    wait(w.at[:, pl.ds(0, NY - 1)], s_wy)
    wait(qn.at[:, pl.ds(0, NX - 1)], s_q)
    wait(ryr, s_ry)
    wait(rzr, s_rz)
    wait(az1.at[:, pl.ds(0, NZ - 1)], s_az)
    wait(wu.at[:, 0, pl.ds(0, NY - 1)], s_ay)
    wait(wu.at[:, 0], s_ac)
    wait(pr, s_p)

    result = att[...]
    for half in range(2):
        wait(pr.at[half], r_p.at[half])
        for k in range(NX - 1):
            result = result + pr[half, k].astype(F32)
    out_ref[...] = result.astype(BF16)


def body(key_tokens, value_tokens, queries, token_rate, fast_weights):
    vmem = pltpu.VMEM
    dma = pltpu.SemaphoreType.DMA
    return pl.pallas_call(
        kernel,
        name="ttt_layer",
        out_shape=jax.ShapeDtypeStruct((TOK, D), BF16),
        in_specs=[pl.BlockSpec(memory_space=pl.ANY)] * 5,
        out_specs=pl.BlockSpec(memory_space=pltpu.VMEM),
        scratch_shapes=[
            vmem((TOK, D), BF16),
            vmem((TOK, D), BF16),
            vmem((TOK, D), BF16),
            vmem((1, TOK), F32),
            vmem((3, ROWS, D), BF16),
            vmem((3, PACK, 128), F32),
            vmem((3, NZ, PACK, 128), BF16),
            vmem((3, NY, BLK, D), BF16),
            vmem((2, 2 * NX, TOK, D), BF16),
            vmem((2, NX, TOK, D), BF16),
            vmem((2, NX, NY * BLK, 2 * TOK), F32),
            vmem((3, NX, NY * BLK, 2 * TOK), BF16),
            vmem((3, NY, BLK, D), BF16),
            vmem((3, NY - 1, BLK, D), BF16),
            vmem((3, NZ, PACK, 128), BF16),
            vmem((3, NZ - 1, PACK, 128), BF16),
            vmem((3, NZ, PACK, 128), BF16),
            vmem((3, 2, NY, BLK, D), BF16),
            vmem((3, 6, BLK + 8, 128), F32),
            vmem((2, 2, NX * TOK, NY * BLK), F32),
            vmem((2, NX, TOK, NY * BLK), BF16),
            vmem((2, NX - 1, TOK, D), BF16),
            vmem((2, NX - 1, TOK, D), BF16),
            vmem((TOK, D), F32),
            dma((5,)), dma, dma((3,)), dma, dma((3,)), dma, dma((3, 2)), dma((NX, 2)), dma, dma((2,)),
            dma, dma((3,)), dma, dma((3,)), dma, dma((3,)), dma, dma((3,)), dma, dma((3,)),
            dma, dma((2,)),
        ],
        compiler_params=pltpu.CompilerParams(
            collective_id=0, has_side_effects=True, vmem_limit_bytes=56 << 20
        ),
    )(key_tokens, value_tokens, queries, token_rate.reshape(1, TOK), fast_weights)


def solution(mesh):
    rows = P(("grp", "dev"), None)
    in_specs = (rows, rows, rows, P(("grp", "dev")), P(None, ("grp", "dev"), None))
    return jax.shard_map(body, mesh=mesh, in_specs=in_specs, out_specs=rows, check_vma=False)
```

```python
import functools

import jax
import jax.numpy as jnp
from jax import lax
from jax.experimental import pallas as pl
from jax.experimental.pallas import tpu as pltpu
from jax.sharding import PartitionSpec as P

D = 768
TOK = 128
EPS = 1e-06
NX, NY, NZ = 4, 4, 8
ROWS = 6
BLK = NZ * ROWS
PACK = 48
HALF = D // 2
MESH = pl.DeviceIdType.MESH
F32 = jnp.float32
BF16 = jnp.bfloat16


def dot_nt(a, b):
    return lax.dot_general(a, b, (((1,), (1,)), ((), ())), preferred_element_type=F32)


def dot_nn(a, b):
    return lax.dot_general(a, b, (((1,), (0,)), ((), ())), preferred_element_type=F32)


def device(x, y, z, c):
    return ((z // 4) * 2 + c, (z % 4) * 16 + y * 4 + x)


def rms_scale(rows):
    return lax.rsqrt(jnp.mean(rows * rows, axis=-1, keepdims=True) + EPS)


def kernel(
    key_hbm, val_hbm, qry_hbm, rate_hbm, w_hbm, out_ref,
    key_ref, val_ref, qry_ref, rate_ref, w_ref,
    wpk, az0, w, ks, qn, gs, act, rys, ryv, rym, ryr, rzs, rzr, az1, wu, unp, gu, hid_q, ps, pv, pm, pr, att,
    s_in, s_az0, r_az0, s_wy, r_wy, s_tok, r_tok, r_tokc, s_q, r_q,
    s_ry, r_ryv, r_ry, s_rz, r_rz, s_az, r_az, s_ay, r_ay, s_ac, r_ac, s_p, r_pv, r_p,
):
    g = lax.axis_index("grp")
    d = lax.axis_index("dev")
    x, y, z, c = d % 4, (d // 4) % 4, (g // 2) * 4 + d // 16, g % 2
    other = device(x, y, z, 1 - c)
    xs = [device((x + k) % NX, y, z, c) for k in range(NX)]
    ys = [device(x, (y + k) % NY, z, c) for k in range(NY)]
    zs = [device(x, y, (z + k) % NZ, c) for k in range(NZ)]
    pos = (y * (1 - c) + x * c, x * (1 - c) + y * c)
    lines = (
        [device((x + k * c) % NX, (y + k * (1 - c)) % NY, z, c) for k in range(NX)],
        [device((x + k * (1 - c)) % NX, (y + k * c) % NY, z, c) for k in range(NX)],
    )
    far_first_z = (4, 3, 5, 2, 6, 1, 7)

    barrier = pltpu.get_barrier_semaphore()
    peers = [other] + xs[1:] + ys[1:] + zs[1:]
    for peer in peers:
        pl.semaphore_signal(barrier, inc=1, device_id=peer, device_id_type=MESH)

    fetches = [
        pltpu.make_async_copy(src, dst, s_in.at[i])
        for i, (src, dst) in enumerate(
            [(w_hbm, w_ref), (key_hbm, key_ref), (val_hbm, val_ref), (rate_hbm, rate_ref), (qry_hbm, qry_ref)]
        )
    ]
    for fetch in fetches:
        fetch.start()

    def send(src, dst, ssem, rsem, peer):
        pltpu.make_async_remote_copy(
            src_ref=src, dst_ref=dst, send_sem=ssem, recv_sem=rsem, device_id=peer, device_id_type=MESH
        ).start()

    def wait(ref, sem):
        pltpu.make_async_copy(ref, ref, sem).wait()

    first, second = pl.ds(0, HALF), pl.ds(HALF, HALF)

    def spread(right1, far, left1, via, got, ssem, via_sem, got_sem, right, left):
        send(far.at[:, first], via.at[0], ssem, via_sem.at[0], right)
        send(far.at[:, second], via.at[1], ssem, via_sem.at[1], left)
        send(right1.at[:, second], got.at[0, :, second], ssem, got_sem, right)
        send(left1.at[:, first], got.at[1, :, first], ssem, got_sem, left)

    def hand_on(right1, left1, via, summed, got, ssem, via_sem, got_sem, right, left):
        wait(via.at[0], via_sem.at[0])
        summed[0] = (right1[:, :HALF].astype(F32) + via[0].astype(F32)).astype(BF16)
        send(summed.at[0], got.at[0, :, first], ssem, got_sem, right)
        wait(via.at[1], via_sem.at[1])
        summed[1] = (left1[:, HALF:].astype(F32) + via[1].astype(F32)).astype(BF16)
        send(summed.at[1], got.at[1, :, second], ssem, got_sem, left)

    wpk[...] = jnp.zeros_like(wpk)
    fetches[0].wait()
    for m in range(3):
        rows = w_ref[m].astype(F32)
        for j in range(6):
            wpk[m, j * 8 : j * 8 + ROWS, :] = rows[:, j * 128 : (j + 1) * 128]
        az0[m, z] = wpk[m].astype(BF16)

    slot = x * 2 + c
    fetches[1].wait()
    keys = key_ref[...].astype(F32)
    ks[0, slot] = (keys * rms_scale(keys)).astype(BF16)
    fetches[2].wait()
    fetches[3].wait()
    diagonal = lax.broadcasted_iota(jnp.int32, (TOK, TOK), 0) == lax.broadcasted_iota(jnp.int32, (TOK, TOK), 1)
    rate = jnp.sum(jnp.where(diagonal, rate_ref[...], 0.0), axis=-1, keepdims=True)
    ks[1, slot] = (-(rate * val_ref[...].astype(F32))).astype(BF16)

    fetches[4].wait()
    queries = qry_ref[...].astype(F32)
    normed = (queries * rms_scale(queries)).astype(BF16)
    qn[0, x] = normed
    qn[1, y] = normed

    pl.semaphore_wait(barrier, len(peers))

    def send_tok(kind, sl, sem, peer):
        send(ks.at[kind, sl], ks.at[kind, sl], s_tok, sem, peer)
    for k in far_first_z:
        send(az0.at[0, z], az0.at[0, z], s_az0, r_az0.at[0], zs[k])
    send_tok(0, slot, r_tok.at[0, 0], xs[1])
    send_tok(1, slot, r_tok.at[2, 1], xs[3])
    send_tok(1, slot, r_tok.at[0, 1], xs[1])
    send_tok(0, slot, r_tok.at[2, 0], xs[3])
    for kind in range(2):
        send_tok(kind, slot, r_tokc.at[0, kind], other)
    for k in (2, 1, 3):
        send(qn.at[1, y], qn.at[1, y], s_q, r_q.at[1], ys[k])
    for m in (1, 2):
        for k in far_first_z:
            send(az0.at[m, z], az0.at[m, z], s_az0, r_az0.at[m], zs[k])

    def token_slot(k, core):
        return ((x + NX - k) % NX) * 2 + core

    def tokens_in(k, kind, onward):
        sl = token_slot(k, c)
        wait(ks.at[kind, sl], r_tok.at[k - 1, kind])
        if onward is not None:
            send_tok(kind, sl, r_tok.at[1, kind], onward)
        send_tok(kind, sl, r_tokc.at[k, kind], other)

    def unpack(m, packed, store):
        for zz in range(NZ):
            unp[m, :, zz * ROWS : zz * ROWS + 8, :] = packed[m, zz].astype(F32).reshape(6, 8, 128)
        for j in range(6):
            store(j, unp[m, j, :BLK, :].astype(BF16))

    def old_weights(m):
        wait(az0.at[m, pl.ds(0, NZ - 1)], r_az0.at[m])
        def put(j, v):
            w[m, y, :, j * 128 : (j + 1) * 128] = v
        unpack(m, az0, put)
        for k in (2, 1, 3):
            send(w.at[m, y], w.at[m, y], s_wy, r_wy.at[m], ys[k])

    old_weights(0)
    old_weights(1)
    tokens_in(1, 0, xs[1])
    tokens_in(3, 1, xs[3])
    old_weights(2)

    lane = lax.broadcasted_iota(jnp.int32, (TOK, 128), 1)
    for p in range(6):
        cols = slice(p * 128, (p + 1) * 128)
        qp, kp, vp = qry_ref[:, cols], key_ref[:, cols], val_ref[:, cols]
        zero = jnp.zeros_like(qp)
        both = jnp.concatenate([jnp.where(lane < 64, qp, zero), jnp.where(lane < 64, zero, qp)], axis=0)
        scores = dot_nt(both, kp) * 0.125
        e = jnp.exp(scores - jnp.max(scores, axis=-1, keepdims=True))
        probs = (e / jnp.sum(e, axis=-1, keepdims=True)).astype(BF16)
        mixed = dot_nn(probs, vp)
        att[:, cols] = jnp.where(lane < 64, mixed[:TOK], mixed[TOK:])

    tokens_in(1, 1, None)
    tokens_in(3, 0, None)

    def chunk(kind, k):
        xx = (x + NX - k) % NX
        return ks[kind, pl.ds(xx * 2, 2)].reshape(2 * TOK, D)

    def forward(k):
        wait(ks.at[0, 0], r_tokc.at[k, 0])
        kn = chunk(0, k)
        gate = dot_nt(w[0].reshape(NY * BLK, D), kn)
        up = dot_nt(w[1].reshape(NY * BLK, D), kn)
        gs[0, k] = gate
        gs[1, k] = up
        act[2, k] = (gate * jax.nn.sigmoid(gate) * up).astype(BF16)

    def backward(k):
        hgrad = dot_nt(w[2].reshape(NY * BLK, D), chunk(1, k))
        gate, up = gs[0, k], gs[1, k]
        sig = jax.nn.sigmoid(gate)
        act[0, k] = (hgrad * up * sig * (1.0 + gate * (1.0 - sig))).astype(BF16)
        act[1, k] = (hgrad * (gate * sig)).astype(BF16)

    wait(w.at[0, pl.ds(0, NY - 1)], r_wy.at[0])
    wait(w.at[1, pl.ds(0, NY - 1)], r_wy.at[1])
    for k in (0, 1, 3):
        forward(k)
    tokens_in(2, 0, None)
    tokens_in(2, 1, None)
    for k in (2, 1, 3):
        send(qn.at[0, x], qn.at[0, x], s_q, r_q.at[0], xs[k])
    forward(2)
    for k in (0, 1, 3, 2):
        wait(ks.at[1, 0], r_tokc.at[k, 1])

    def gradient(m):
        total = None
        for k in range(NX):
            term = dot_nn(act[m, k], chunk(1 if m == 2 else 0, k))
            total = term if total is None else total + term
        rys[m] = total.astype(BF16).reshape(NY, BLK, D)
        spread(
            rys.at[m, (y + 1) % NY], rys.at[m, (y + 2) % NY], rys.at[m, (y + 3) % NY], ryv.at[m], ryr.at[m],
            s_ry, r_ryv.at[m], r_ry.at[m], ys[1], ys[3],
        )

    gradient(2)
    wait(w.at[2, pl.ds(0, NY - 1)], r_wy.at[2])
    for k in (0, 1, 3, 2):
        backward(k)
    gradient(0)
    gradient(1)

    order = (2, 0, 1)
    for m in order:
        hand_on(
            rys.at[m, (y + 1) % NY], rys.at[m, (y + 3) % NY], ryv.at[m], rym.at[m], ryr.at[m],
            s_ry, r_ryv.at[m], r_ry.at[m], ys[1], ys[3],
        )
    unp[:, :, BLK:, :] = jnp.zeros((3, 6, 8, 128), F32)
    for m in order:
        wait(ryr.at[m], r_ry.at[m])
        total = rys[m, y].astype(F32)
        total = total + ryr[m, 0].astype(F32) + ryr[m, 1].astype(F32)
        for j in range(6):
            unp[m, j, :BLK, :] = total[:, j * 128 : (j + 1) * 128]
        for zz in range(NZ):
            rzs[m, zz] = unp[m, :, zz * ROWS : zz * ROWS + 8, :].reshape(PACK, 128).astype(BF16)
        for k in far_first_z:
            send(rzs.at[m, (z + k) % NZ], rzr.at[m, k - 1], s_rz, r_rz.at[m], zs[k])

    for m in order:
        wait(rzr.at[m], r_rz.at[m])
        grad = rzs[m, z].astype(F32)
        for k in range(NZ - 1):
            grad = grad + rzr[m, k].astype(F32)
        old = wpk[m].reshape(6, 8, 128)
        stepped = old - grad.reshape(6, 8, 128)
        old_ms = jnp.sum(jnp.sum(old * old, axis=0), axis=-1, keepdims=True) * (1.0 / D)
        new_ms = jnp.sum(jnp.sum(stepped * stepped, axis=0), axis=-1, keepdims=True) * (1.0 / D)
        upd = stepped * jnp.sqrt(old_ms + EPS)[None] / jnp.sqrt(new_ms + EPS)[None]
        az1[m, z] = upd.reshape(PACK, 128).astype(BF16)
        for k in far_first_z:
            send(az1.at[m, z], az1.at[m, z], s_az, r_az.at[m], zs[k])

    for m in order:
        wait(az1.at[m, pl.ds(0, NZ - 1)], r_az.at[m])
        def put_new(j, v, m=m):
            wu[m, c, pos[0], :, j * 128 : (j + 1) * 128] = v
        unpack(m, az1, put_new)
        for k in (2, 1, 3):
            send(wu.at[m, c, pos[0]], wu.at[m, c, pos[0]], s_ay, r_ay.at[m], lines[0][k])

    def project(m, half, core):
        gu[m, half] = dot_nt(qn[core].reshape(NX * TOK, D), wu[m, core].reshape(NY * BLK, D))

    def query_hidden(half):
        gate = gu[0, half]
        hid_q[half] = (gate * jax.nn.sigmoid(gate) * gu[1, half]).astype(BF16).reshape(NX, TOK, NY * BLK)

    def partial_outputs(half, core):
        down = wu[2, core].reshape(NY * BLK, D)
        for k in (2, 1, 3):
            ps[half, k - 1] = dot_nn(hid_q[half, (pos[1 - half] + k) % NX], down).astype(BF16)
        spread(
            ps.at[half, 0], ps.at[half, 1], ps.at[half, 2], pv.at[half], pr.at[half],
            s_p, r_pv.at[half], r_p.at[half], lines[1 - half][1], lines[1 - half][3],
        )
        att[...] += dot_nn(hid_q[half, pos[1 - half]], down)

    for axis in range(2):
        wait(qn.at[axis, pl.ds(0, NX - 1)], r_q.at[axis])
    for m in order:
        wait(wu.at[m, c, pl.ds(0, NY - 1)], r_ay.at[m])
        send(wu.at[m, c], wu.at[m, c], s_ac, r_ac.at[m], other)
        if m < 2:
            project(m, 0, c)
    query_hidden(0)
    partial_outputs(0, c)
    for m in (0, 1):
        wait(wu.at[m, 1 - c], r_ac.at[m])
        project(m, 1, 1 - c)
    query_hidden(1)
    wait(wu.at[2, 1 - c], r_ac.at[2])
    partial_outputs(1, 1 - c)
    for half in range(2):
        hand_on(
            ps.at[half, 0], ps.at[half, 2], pv.at[half], pm.at[half], pr.at[half],
            s_p, r_pv.at[half], r_p.at[half], lines[1 - half][1], lines[1 - half][3],
        )

    wait(az0.at[:, pl.ds(0, NZ - 1)], s_az0)
    for _ in range(7):
        wait(ks.at[:, 0], s_tok)
    wait(w.at[:, pl.ds(0, NY - 1)], s_wy)
    wait(qn.at[:, pl.ds(0, NX - 1)], s_q)
    wait(rys.at[:, pl.ds(0, NY - 1)], s_ry)
    wait(rzr, s_rz)
    wait(az1.at[:, pl.ds(0, NZ - 1)], s_az)
    wait(wu.at[:, 0, pl.ds(0, NY - 1)], s_ay)
    wait(wu.at[:, 0], s_ac)
    wait(ps, s_p)

    result = att[...]
    for half in range(2):
        wait(pr.at[half], r_p.at[half])
        result = result + pr[half, 0].astype(F32) + pr[half, 1].astype(F32)
    out_ref[...] = result.astype(BF16)


def body(key_tokens, value_tokens, queries, token_rate, fast_weights):
    vmem = pltpu.VMEM
    dma = pltpu.SemaphoreType.DMA
    return pl.pallas_call(
        kernel,
        name="ttt_layer",
        out_shape=jax.ShapeDtypeStruct((TOK, D), BF16),
        in_specs=[pl.BlockSpec(memory_space=pl.ANY)] * 5,
        out_specs=pl.BlockSpec(memory_space=pltpu.VMEM),
        scratch_shapes=[
            vmem((TOK, D), BF16),
            vmem((TOK, D), BF16),
            vmem((TOK, D), BF16),
            vmem((1, TOK), F32),
            vmem((3, ROWS, D), BF16),
            vmem((3, PACK, 128), F32),
            vmem((3, NZ, PACK, 128), BF16),
            vmem((3, NY, BLK, D), BF16),
            vmem((2, 2 * NX, TOK, D), BF16),
            vmem((2, NX, TOK, D), BF16),
            vmem((2, NX, NY * BLK, 2 * TOK), F32),
            vmem((3, NX, NY * BLK, 2 * TOK), BF16),
            vmem((3, NY, BLK, D), BF16),
            vmem((3, 2, BLK, HALF), BF16),
            vmem((3, 2, BLK, HALF), BF16),
            vmem((3, 2, BLK, D), BF16),
            vmem((3, NZ, PACK, 128), BF16),
            vmem((3, NZ - 1, PACK, 128), BF16),
            vmem((3, NZ, PACK, 128), BF16),
            vmem((3, 2, NY, BLK, D), BF16),
            vmem((3, 6, BLK + 8, 128), F32),
            vmem((2, 2, NX * TOK, NY * BLK), F32),
            vmem((2, NX, TOK, NY * BLK), BF16),
            vmem((2, NX - 1, TOK, D), BF16),
            vmem((2, 2, TOK, HALF), BF16),
            vmem((2, 2, TOK, HALF), BF16),
            vmem((2, 2, TOK, D), BF16),
            vmem((TOK, D), F32),
            dma((5,)), dma, dma((3,)), dma, dma((3,)), dma, dma((3, 2)), dma((NX, 2)), dma, dma((2,)),
            dma, dma((3, 2)), dma((3,)), dma, dma((3,)), dma, dma((3,)), dma, dma((3,)), dma, dma((3,)),
            dma, dma((2, 2)), dma((2,)),
        ],
        compiler_params=pltpu.CompilerParams(
            collective_id=0, has_side_effects=True, vmem_limit_bytes=56 << 20
        ),
    )(key_tokens, value_tokens, queries, token_rate.reshape(1, TOK), fast_weights)


def solution(mesh):
    rows = P(("grp", "dev"), None)
    in_specs = (rows, rows, rows, P(("grp", "dev")), P(None, ("grp", "dev"), None))
    return jax.shard_map(body, mesh=mesh, in_specs=in_specs, out_specs=rows, check_vma=False)
```

```python
import functools

import jax
import jax.numpy as jnp
from jax import lax
from jax.experimental import pallas as pl
from jax.experimental.pallas import tpu as pltpu
from jax.sharding import PartitionSpec as P

D = 768
TOK = 128
EPS = 1e-06
NX, NY, NZ = 4, 4, 8
ROWS = 6
BLK = NZ * ROWS
PACK = 48
HALF = D // 2
MESH = pl.DeviceIdType.MESH
F32 = jnp.float32
BF16 = jnp.bfloat16


def dot_nt(a, b):
    return lax.dot_general(a, b, (((1,), (1,)), ((), ())), preferred_element_type=F32)


def dot_nn(a, b):
    return lax.dot_general(a, b, (((1,), (0,)), ((), ())), preferred_element_type=F32)


def device(x, y, z, c):
    return ((z // 4) * 2 + c, (z % 4) * 16 + y * 4 + x)


def rms_scale(rows):
    return lax.rsqrt(jnp.mean(rows * rows, axis=-1, keepdims=True) + EPS)


def kernel(
    key_hbm, val_hbm, qry_hbm, rate_hbm, w_hbm, out_ref,
    key_ref, val_ref, qry_ref, rate_ref, w_ref,
    wpk, az0, w, ks, qn, gs, act, rys, ryv, rym, ryr, rzs, rzr, az1, wu, unp, gu, hid_q, ps, pv, pm, pr, att,
    s_in, s_az0, r_az0, s_wy, r_wy, s_tok, r_tok, r_tokc, s_q, r_q,
    s_ry, r_ryv, r_ry, s_rz, r_rz, s_az, r_az, s_ay, r_ay, s_ac, r_ac, s_p, r_pv, r_p,
):
    g = lax.axis_index("grp")
    d = lax.axis_index("dev")
    x, y, z, c = d % 4, (d // 4) % 4, (g // 2) * 4 + d // 16, g % 2
    other = device(x, y, z, 1 - c)
    xs = [device((x + k) % NX, y, z, c) for k in range(NX)]
    ys = [device(x, (y + k) % NY, z, c) for k in range(NY)]
    zs = [device(x, y, (z + k) % NZ, c) for k in range(NZ)]
    pos = (y * (1 - c) + x * c, x * (1 - c) + y * c)
    lines = (
        [device((x + k * c) % NX, (y + k * (1 - c)) % NY, z, c) for k in range(NX)],
        [device((x + k * (1 - c)) % NX, (y + k * c) % NY, z, c) for k in range(NX)],
    )
    far_first_z = (4, 3, 5, 2, 6, 1, 7)

    barrier = pltpu.get_barrier_semaphore()
    peers = [other] + xs[1:] + ys[1:] + zs[1:]
    for peer in peers:
        pl.semaphore_signal(barrier, inc=1, device_id=peer, device_id_type=MESH)

    fetches = [
        pltpu.make_async_copy(src, dst, s_in.at[i])
        for i, (src, dst) in enumerate(
            [(w_hbm, w_ref), (key_hbm, key_ref), (val_hbm, val_ref), (rate_hbm, rate_ref), (qry_hbm, qry_ref)]
        )
    ]
    for fetch in fetches:
        fetch.start()

    def send(src, dst, ssem, rsem, peer):
        pltpu.make_async_remote_copy(
            src_ref=src, dst_ref=dst, send_sem=ssem, recv_sem=rsem, device_id=peer, device_id_type=MESH
        ).start()

    def wait(ref, sem):
        pltpu.make_async_copy(ref, ref, sem).wait()

    first, second = pl.ds(0, HALF), pl.ds(HALF, HALF)

    def spread(right1, far, left1, via, got, ssem, via_sem, got_sem, right, left):
        send(far.at[:, first], via.at[0], ssem, via_sem.at[0], right)
        send(far.at[:, second], via.at[1], ssem, via_sem.at[1], left)
        send(right1.at[:, second], got.at[0, :, second], ssem, got_sem, right)
        send(left1.at[:, first], got.at[1, :, first], ssem, got_sem, left)

    def hand_on(right1, left1, via, summed, got, ssem, via_sem, got_sem, right, left):
        wait(via.at[0], via_sem.at[0])
        summed[0] = (right1[:, :HALF].astype(F32) + via[0].astype(F32)).astype(BF16)
        send(summed.at[0], got.at[0, :, first], ssem, got_sem, right)
        wait(via.at[1], via_sem.at[1])
        summed[1] = (left1[:, HALF:].astype(F32) + via[1].astype(F32)).astype(BF16)
        send(summed.at[1], got.at[1, :, second], ssem, got_sem, left)

    wpk[...] = jnp.zeros_like(wpk)
    fetches[0].wait()
    for m in range(3):
        rows = w_ref[m].astype(F32)
        for j in range(6):
            wpk[m, j * 8 : j * 8 + ROWS, :] = rows[:, j * 128 : (j + 1) * 128]
        az0[m, z] = wpk[m].astype(BF16)

    slot = x * 2 + c
    fetches[1].wait()
    keys = key_ref[...].astype(F32)
    ks[0, slot] = (keys * rms_scale(keys)).astype(BF16)
    fetches[2].wait()
    fetches[3].wait()
    diagonal = lax.broadcasted_iota(jnp.int32, (TOK, TOK), 0) == lax.broadcasted_iota(jnp.int32, (TOK, TOK), 1)
    rate = jnp.sum(jnp.where(diagonal, rate_ref[...], 0.0), axis=-1, keepdims=True)
    ks[1, slot] = (-(rate * val_ref[...].astype(F32))).astype(BF16)

    fetches[4].wait()
    queries = qry_ref[...].astype(F32)
    normed = (queries * rms_scale(queries)).astype(BF16)
    qn[0, x] = normed
    qn[1, y] = normed

    pl.semaphore_wait(barrier, len(peers))

    def send_tok(kind, sl, sem, peer):
        send(ks.at[kind, sl], ks.at[kind, sl], s_tok, sem, peer)
    for k in far_first_z:
        send(az0.at[0, z], az0.at[0, z], s_az0, r_az0.at[0], zs[k])
    send_tok(0, slot, r_tok.at[0, 0], xs[1])
    send_tok(1, slot, r_tok.at[2, 1], xs[3])
    send_tok(1, slot, r_tok.at[0, 1], xs[1])
    send_tok(0, slot, r_tok.at[2, 0], xs[3])
    for kind in range(2):
        send_tok(kind, slot, r_tokc.at[0, kind], other)
    for k in (1, 3):
        send(qn.at[1, y], qn.at[1, y], s_q, r_q.at[1, k - 1], ys[k])
    for m in (1, 2):
        for k in far_first_z:
            send(az0.at[m, z], az0.at[m, z], s_az0, r_az0.at[m], zs[k])

    def token_slot(k, core):
        return ((x + NX - k) % NX) * 2 + core

    def tokens_in(k, kind, onward):
        sl = token_slot(k, c)
        wait(ks.at[kind, sl], r_tok.at[k - 1, kind])
        if onward is not None:
            send_tok(kind, sl, r_tok.at[1, kind], onward)
        send_tok(kind, sl, r_tokc.at[k, kind], other)

    def unpack(m, packed, store):
        for zz in range(NZ):
            unp[m, :, zz * ROWS : zz * ROWS + 8, :] = packed[m, zz].astype(F32).reshape(6, 8, 128)
        for j in range(6):
            store(j, unp[m, j, :BLK, :].astype(BF16))

    def old_weights(m):
        wait(az0.at[m, pl.ds(0, NZ - 1)], r_az0.at[m])
        def put(j, v):
            w[m, y, :, j * 128 : (j + 1) * 128] = v
        unpack(m, az0, put)
        for k in (2, 1, 3):
            send(w.at[m, y], w.at[m, y], s_wy, r_wy.at[m], ys[k])

    old_weights(0)
    old_weights(1)
    tokens_in(1, 0, xs[1])
    tokens_in(3, 1, xs[3])
    old_weights(2)

    lane = lax.broadcasted_iota(jnp.int32, (TOK, 128), 1)
    for p in range(6):
        cols = slice(p * 128, (p + 1) * 128)
        qp, kp, vp = qry_ref[:, cols], key_ref[:, cols], val_ref[:, cols]
        zero = jnp.zeros_like(qp)
        both = jnp.concatenate([jnp.where(lane < 64, qp, zero), jnp.where(lane < 64, zero, qp)], axis=0)
        scores = dot_nt(both, kp) * 0.125
        e = jnp.exp(scores - jnp.max(scores, axis=-1, keepdims=True))
        probs = (e / jnp.sum(e, axis=-1, keepdims=True)).astype(BF16)
        mixed = dot_nn(probs, vp)
        att[:, cols] = jnp.where(lane < 64, mixed[:TOK], mixed[TOK:])

    tokens_in(1, 1, None)
    tokens_in(3, 0, None)

    def chunk(kind, k):
        xx = (x + NX - k) % NX
        return ks[kind, pl.ds(xx * 2, 2)].reshape(2 * TOK, D)

    def forward(k):
        wait(ks.at[0, 0], r_tokc.at[k, 0])
        kn = chunk(0, k)
        gate = dot_nt(w[0].reshape(NY * BLK, D), kn)
        up = dot_nt(w[1].reshape(NY * BLK, D), kn)
        gs[0, k] = gate
        gs[1, k] = up
        act[2, k] = (gate * jax.nn.sigmoid(gate) * up).astype(BF16)

    def backward(k):
        hgrad = dot_nt(w[2].reshape(NY * BLK, D), chunk(1, k))
        gate, up = gs[0, k], gs[1, k]
        sig = jax.nn.sigmoid(gate)
        act[0, k] = (hgrad * up * sig * (1.0 + gate * (1.0 - sig))).astype(BF16)
        act[1, k] = (hgrad * (gate * sig)).astype(BF16)

    wait(w.at[0, pl.ds(0, NY - 1)], r_wy.at[0])
    wait(w.at[1, pl.ds(0, NY - 1)], r_wy.at[1])
    for k in (0, 1, 3):
        forward(k)
    tokens_in(2, 0, None)
    tokens_in(2, 1, None)
    for k in (2, 1, 3):
        send(qn.at[0, x], qn.at[0, x], s_q, r_q.at[0, k - 1], xs[k])
    forward(2)
    for k in (0, 1, 3, 2):
        wait(ks.at[1, 0], r_tokc.at[k, 1])

    def gradient(m):
        total = None
        for k in range(NX):
            term = dot_nn(act[m, k], chunk(1 if m == 2 else 0, k))
            total = term if total is None else total + term
        rys[m] = total.astype(BF16).reshape(NY, BLK, D)
        spread(
            rys.at[m, (y + 1) % NY], rys.at[m, (y + 2) % NY], rys.at[m, (y + 3) % NY], ryv.at[m], ryr.at[m],
            s_ry, r_ryv.at[m], r_ry.at[m], ys[1], ys[3],
        )

    wait(w.at[2, pl.ds(0, NY - 1)], r_wy.at[2])
    for k in (0, 1, 3, 2):
        backward(k)
    order = (0, 1, 2)
    for m in order:
        gradient(m)
    for m in order:
        hand_on(
            rys.at[m, (y + 1) % NY], rys.at[m, (y + 3) % NY], ryv.at[m], rym.at[m], ryr.at[m],
            s_ry, r_ryv.at[m], r_ry.at[m], ys[1], ys[3],
        )

    above, below = (y + NY - 1) % NY, (y + 1) % NY
    wait(qn.at[1, above], r_q.at[1, 0])
    send(qn.at[1, above, :, first], qn.at[1, above, :, first], s_q, r_q.at[1, 1], ys[1])
    wait(qn.at[1, below], r_q.at[1, 2])
    send(qn.at[1, below, :, second], qn.at[1, below, :, second], s_q, r_q.at[1, 1], ys[3])

    unp[:, :, BLK:, :] = jnp.zeros((3, 6, 8, 128), F32)
    for m in order:
        wait(ryr.at[m], r_ry.at[m])
        total = rys[m, y].astype(F32)
        total = total + ryr[m, 0].astype(F32) + ryr[m, 1].astype(F32)
        for j in range(6):
            unp[m, j, :BLK, :] = total[:, j * 128 : (j + 1) * 128]
        for zz in range(NZ):
            rzs[m, zz] = unp[m, :, zz * ROWS : zz * ROWS + 8, :].reshape(PACK, 128).astype(BF16)
        for k in far_first_z:
            send(rzs.at[m, (z + k) % NZ], rzr.at[m, k - 1], s_rz, r_rz.at[m], zs[k])

    for m in order:
        wait(rzr.at[m], r_rz.at[m])
        grad = rzs[m, z].astype(F32)
        for k in range(NZ - 1):
            grad = grad + rzr[m, k].astype(F32)
        old = wpk[m].reshape(6, 8, 128)
        stepped = old - grad.reshape(6, 8, 128)
        old_ms = jnp.sum(jnp.sum(old * old, axis=0), axis=-1, keepdims=True) * (1.0 / D)
        new_ms = jnp.sum(jnp.sum(stepped * stepped, axis=0), axis=-1, keepdims=True) * (1.0 / D)
        upd = stepped * jnp.sqrt(old_ms + EPS)[None] / jnp.sqrt(new_ms + EPS)[None]
        az1[m, z] = upd.reshape(PACK, 128).astype(BF16)
        for k in far_first_z:
            send(az1.at[m, z], az1.at[m, z], s_az, r_az.at[m], zs[k])

    for m in order:
        wait(az1.at[m, pl.ds(0, NZ - 1)], r_az.at[m])
        def put_new(j, v, m=m):
            wu[m, c, pos[0], :, j * 128 : (j + 1) * 128] = v
        unpack(m, az1, put_new)
        for k in (2, 1, 3):
            send(wu.at[m, c, pos[0]], wu.at[m, c, pos[0]], s_ay, r_ay.at[m], lines[0][k])

    def project(m, half, core):
        gu[m, half] = dot_nt(qn[core].reshape(NX * TOK, D), wu[m, core].reshape(NY * BLK, D))

    def query_hidden(half):
        gate = gu[0, half]
        hid_q[half] = (gate * jax.nn.sigmoid(gate) * gu[1, half]).astype(BF16).reshape(NX, TOK, NY * BLK)

    def partial_outputs(half, core):
        down = wu[2, core].reshape(NY * BLK, D)
        for k in (2, 1, 3):
            ps[half, k - 1] = dot_nn(hid_q[half, (pos[1 - half] + k) % NX], down).astype(BF16)
        spread(
            ps.at[half, 0], ps.at[half, 1], ps.at[half, 2], pv.at[half], pr.at[half],
            s_p, r_pv.at[half], r_p.at[half], lines[1 - half][1], lines[1 - half][3],
        )
        att[...] += dot_nn(hid_q[half, pos[1 - half]], down)

    for k in range(NX - 1):
        wait(qn.at[0, 0], r_q.at[0, k])
    wait(qn.at[1, 0], r_q.at[1, 1])
    for m in order:
        wait(wu.at[m, c, pl.ds(0, NY - 1)], r_ay.at[m])
        send(wu.at[m, c], wu.at[m, c], s_ac, r_ac.at[m], other)
        if m < 2:
            project(m, 0, c)
    query_hidden(0)
    partial_outputs(0, c)
    for m in (0, 1):
        wait(wu.at[m, 1 - c], r_ac.at[m])
        project(m, 1, 1 - c)
    query_hidden(1)
    wait(wu.at[2, 1 - c], r_ac.at[2])
    partial_outputs(1, 1 - c)
    for half in range(2):
        hand_on(
            ps.at[half, 0], ps.at[half, 2], pv.at[half], pm.at[half], pr.at[half],
            s_p, r_pv.at[half], r_p.at[half], lines[1 - half][1], lines[1 - half][3],
        )

    wait(az0.at[:, pl.ds(0, NZ - 1)], s_az0)
    for _ in range(7):
        wait(ks.at[:, 0], s_tok)
    wait(w.at[:, pl.ds(0, NY - 1)], s_wy)
    wait(qn.at[:, pl.ds(0, NX - 1)], s_q)
    wait(rys.at[:, pl.ds(0, NY - 1)], s_ry)
    wait(rzr, s_rz)
    wait(az1.at[:, pl.ds(0, NZ - 1)], s_az)
    wait(wu.at[:, 0, pl.ds(0, NY - 1)], s_ay)
    wait(wu.at[:, 0], s_ac)
    wait(ps, s_p)

    result = att[...]
    for half in range(2):
        wait(pr.at[half], r_p.at[half])
        result = result + pr[half, 0].astype(F32) + pr[half, 1].astype(F32)
    out_ref[...] = result.astype(BF16)


def body(key_tokens, value_tokens, queries, token_rate, fast_weights):
    vmem = pltpu.VMEM
    dma = pltpu.SemaphoreType.DMA
    return pl.pallas_call(
        kernel,
        name="ttt_layer",
        out_shape=jax.ShapeDtypeStruct((TOK, D), BF16),
        in_specs=[pl.BlockSpec(memory_space=pl.ANY)] * 5,
        out_specs=pl.BlockSpec(memory_space=pltpu.VMEM),
        scratch_shapes=[
            vmem((TOK, D), BF16),
            vmem((TOK, D), BF16),
            vmem((TOK, D), BF16),
            vmem((1, TOK), F32),
            vmem((3, ROWS, D), BF16),
            vmem((3, PACK, 128), F32),
            vmem((3, NZ, PACK, 128), BF16),
            vmem((3, NY, BLK, D), BF16),
            vmem((2, 2 * NX, TOK, D), BF16),
            vmem((2, NX, TOK, D), BF16),
            vmem((2, NX, NY * BLK, 2 * TOK), F32),
            vmem((3, NX, NY * BLK, 2 * TOK), BF16),
            vmem((3, NY, BLK, D), BF16),
            vmem((3, 2, BLK, HALF), BF16),
            vmem((3, 2, BLK, HALF), BF16),
            vmem((3, 2, BLK, D), BF16),
            vmem((3, NZ, PACK, 128), BF16),
            vmem((3, NZ - 1, PACK, 128), BF16),
            vmem((3, NZ, PACK, 128), BF16),
            vmem((3, 2, NY, BLK, D), BF16),
            vmem((3, 6, BLK + 8, 128), F32),
            vmem((2, 2, NX * TOK, NY * BLK), F32),
            vmem((2, NX, TOK, NY * BLK), BF16),
            vmem((2, NX - 1, TOK, D), BF16),
            vmem((2, 2, TOK, HALF), BF16),
            vmem((2, 2, TOK, HALF), BF16),
            vmem((2, 2, TOK, D), BF16),
            vmem((TOK, D), F32),
            dma((5,)), dma, dma((3,)), dma, dma((3,)), dma, dma((3, 2)), dma((NX, 2)), dma, dma((2, 3)),
            dma, dma((3, 2)), dma((3,)), dma, dma((3,)), dma, dma((3,)), dma, dma((3,)), dma, dma((3,)),
            dma, dma((2, 2)), dma((2,)),
        ],
        compiler_params=pltpu.CompilerParams(
            collective_id=0, has_side_effects=True, vmem_limit_bytes=56250000
        ),
    )(key_tokens, value_tokens, queries, token_rate.reshape(1, TOK), fast_weights)


def solution(mesh):
    rows = P(("grp", "dev"), None)
    in_specs = (rows, rows, rows, P(("grp", "dev")), P(None, ("grp", "dev"), None))
    return jax.shard_map(body, mesh=mesh, in_specs=in_specs, out_specs=rows, check_vma=False)
```

```python
import functools

import jax
import jax.numpy as jnp
from jax import lax
from jax.experimental import pallas as pl
from jax.experimental.pallas import tpu as pltpu
from jax.sharding import PartitionSpec as P

D = 768
TOK = 128
EPS = 1e-06
NX, NY, NZ = 4, 4, 8
ROWS = 6
BLK = NZ * ROWS
PACK = 48
HALF = D // 2
MESH = pl.DeviceIdType.MESH
F32 = jnp.float32
BF16 = jnp.bfloat16


def dot_nt(a, b):
    return lax.dot_general(a, b, (((1,), (1,)), ((), ())), preferred_element_type=F32)


def dot_nn(a, b):
    return lax.dot_general(a, b, (((1,), (0,)), ((), ())), preferred_element_type=F32)


def device(x, y, z, c):
    return ((z // 4) * 2 + c, (z % 4) * 16 + y * 4 + x)


def rms_scale(rows):
    return lax.rsqrt(jnp.mean(rows * rows, axis=-1, keepdims=True) + EPS)


def kernel(
    key_hbm, val_hbm, qry_hbm, rate_hbm, w_hbm, out_ref,
    key_ref, val_ref, qry_ref, rate_ref, w_ref,
    wpk, az0, w, ks, qn, gs, act, rys, ryv, rym, ryr, rzs, rzr, az1, wu, unp, gu, hid_q, ps, pv, pm, pr, att,
    s_in, s_az0, r_az0, s_wy, r_wy, s_tok, r_tok, r_tokc, s_q, r_q,
    s_ry, r_ryv, r_ry, s_rz, r_rz, s_az, r_az, s_ay, r_ay, s_ac, r_ac, s_p, r_pv, r_p,
):
    g = lax.axis_index("grp")
    d = lax.axis_index("dev")
    x, y, z, c = d % 4, (d // 4) % 4, (g // 2) * 4 + d // 16, g % 2
    other = device(x, y, z, 1 - c)
    xs = [device((x + k) % NX, y, z, c) for k in range(NX)]
    ys = [device(x, (y + k) % NY, z, c) for k in range(NY)]
    zs = [device(x, y, (z + k) % NZ, c) for k in range(NZ)]
    pos = (y * (1 - c) + x * c, x * (1 - c) + y * c)
    lines = (
        [device((x + k * c) % NX, (y + k * (1 - c)) % NY, z, c) for k in range(NX)],
        [device((x + k * (1 - c)) % NX, (y + k * c) % NY, z, c) for k in range(NX)],
    )
    far_first_z = (4, 3, 5, 2, 6, 1, 7)

    barrier = pltpu.get_barrier_semaphore()
    peers = [zs[k] for k in far_first_z] + [ys[2], xs[2], ys[1], ys[3], xs[1], xs[3], other]
    for peer in peers:
        pl.semaphore_signal(barrier, inc=1, device_id=peer, device_id_type=MESH)

    fetches = [
        pltpu.make_async_copy(src, dst, s_in.at[i])
        for i, (src, dst) in enumerate(
            [(w_hbm, w_ref), (key_hbm, key_ref), (val_hbm, val_ref), (rate_hbm, rate_ref), (qry_hbm, qry_ref)]
        )
    ]
    for fetch in fetches:
        fetch.start()

    def send(src, dst, ssem, rsem, peer):
        pltpu.make_async_remote_copy(
            src_ref=src, dst_ref=dst, send_sem=ssem, recv_sem=rsem, device_id=peer, device_id_type=MESH
        ).start()

    def wait(ref, sem):
        pltpu.make_async_copy(ref, ref, sem).wait()

    first, second = pl.ds(0, HALF), pl.ds(HALF, HALF)

    def spread(right1, far, left1, via, got, ssem, via_sem, got_sem, right, left):
        send(far.at[:, first], via.at[0], ssem, via_sem.at[0], right)
        send(far.at[:, second], via.at[1], ssem, via_sem.at[1], left)
        send(right1.at[:, second], got.at[0, :, second], ssem, got_sem, right)
        send(left1.at[:, first], got.at[1, :, first], ssem, got_sem, left)

    def hand_on(right1, left1, via, summed, got, ssem, via_sem, got_sem, right, left):
        wait(via.at[0], via_sem.at[0])
        summed[0] = (right1[:, :HALF].astype(F32) + via[0].astype(F32)).astype(BF16)
        send(summed.at[0], got.at[0, :, first], ssem, got_sem, right)
        wait(via.at[1], via_sem.at[1])
        summed[1] = (left1[:, HALF:].astype(F32) + via[1].astype(F32)).astype(BF16)
        send(summed.at[1], got.at[1, :, second], ssem, got_sem, left)

    wpk[...] = jnp.zeros_like(wpk)
    fetches[0].wait()
    for m in range(3):
        rows = w_ref[m].astype(F32)
        for j in range(6):
            wpk[m, j * 8 : j * 8 + ROWS, :] = rows[:, j * 128 : (j + 1) * 128]
        az0[m, z] = wpk[m].astype(BF16)

    slot = x * 2 + c
    fetches[1].wait()
    keys = key_ref[...].astype(F32)
    ks[0, slot] = (keys * rms_scale(keys)).astype(BF16)
    fetches[2].wait()
    fetches[3].wait()
    diagonal = lax.broadcasted_iota(jnp.int32, (TOK, TOK), 0) == lax.broadcasted_iota(jnp.int32, (TOK, TOK), 1)
    rate = jnp.sum(jnp.where(diagonal, rate_ref[...], 0.0), axis=-1, keepdims=True)
    ks[1, slot] = (-(rate * val_ref[...].astype(F32))).astype(BF16)

    fetches[4].wait()
    queries = qry_ref[...].astype(F32)
    normed = (queries * rms_scale(queries)).astype(BF16)
    qn[0, x] = normed
    qn[1, y] = normed

    pl.semaphore_wait(barrier, len(peers))

    def send_tok(kind, sl, sem, peer):
        send(ks.at[kind, sl], ks.at[kind, sl], s_tok, sem, peer)
    for k in far_first_z:
        send(az0.at[0, z], az0.at[0, z], s_az0, r_az0.at[0], zs[k])
    send_tok(0, slot, r_tok.at[0, 0], xs[1])
    send_tok(1, slot, r_tok.at[2, 1], xs[3])
    send_tok(1, slot, r_tok.at[0, 1], xs[1])
    send_tok(0, slot, r_tok.at[2, 0], xs[3])
    for kind in range(2):
        send_tok(kind, slot, r_tokc.at[0, kind], other)
    for k in (1, 3):
        send(qn.at[1, y], qn.at[1, y], s_q, r_q.at[1, k - 1], ys[k])
    for m in (1, 2):
        for k in far_first_z:
            send(az0.at[m, z], az0.at[m, z], s_az0, r_az0.at[m], zs[k])

    def token_slot(k, core):
        return ((x + NX - k) % NX) * 2 + core

    def tokens_in(k, kind, onward):
        sl = token_slot(k, c)
        wait(ks.at[kind, sl], r_tok.at[k - 1, kind])
        if onward is not None:
            send_tok(kind, sl, r_tok.at[1, kind], onward)
        send_tok(kind, sl, r_tokc.at[k, kind], other)

    def unpack(m, packed, store):
        for zz in range(NZ):
            unp[m, :, zz * ROWS : zz * ROWS + 8, :] = packed[m, zz].astype(F32).reshape(6, 8, 128)
        for j in range(6):
            store(j, unp[m, j, :BLK, :].astype(BF16))

    def old_weights(m):
        wait(az0.at[m, pl.ds(0, NZ - 1)], r_az0.at[m])
        def put(j, v):
            w[m, y, :, j * 128 : (j + 1) * 128] = v
        unpack(m, az0, put)
        for k in (2, 1, 3):
            send(w.at[m, y], w.at[m, y], s_wy, r_wy.at[m], ys[k])

    old_weights(0)
    old_weights(1)
    tokens_in(1, 0, xs[1])
    tokens_in(3, 1, xs[3])
    old_weights(2)

    lane = lax.broadcasted_iota(jnp.int32, (TOK, 128), 1)
    for p in range(6):
        cols = slice(p * 128, (p + 1) * 128)
        qp, kp, vp = qry_ref[:, cols], key_ref[:, cols], val_ref[:, cols]
        zero = jnp.zeros_like(qp)
        both = jnp.concatenate([jnp.where(lane < 64, qp, zero), jnp.where(lane < 64, zero, qp)], axis=0)
        scores = dot_nt(both, kp) * 0.125
        e = jnp.exp(scores - jnp.max(scores, axis=-1, keepdims=True))
        probs = (e / jnp.sum(e, axis=-1, keepdims=True)).astype(BF16)
        mixed = dot_nn(probs, vp)
        att[:, cols] = jnp.where(lane < 64, mixed[:TOK], mixed[TOK:])

    tokens_in(1, 1, None)
    tokens_in(3, 0, None)

    def chunk(kind, k):
        xx = (x + NX - k) % NX
        return ks[kind, pl.ds(xx * 2, 2)].reshape(2 * TOK, D)

    def forward(k):
        wait(ks.at[0, 0], r_tokc.at[k, 0])
        kn = chunk(0, k)
        gate = dot_nt(w[0].reshape(NY * BLK, D), kn)
        up = dot_nt(w[1].reshape(NY * BLK, D), kn)
        sig = jax.nn.sigmoid(gate)
        silu = gate * sig
        act[2, k] = (silu * up).astype(BF16)
        gs[0, k] = up * sig * (1.0 + gate * (1.0 - sig))
        gs[1, k] = silu

    def backward(k):
        hgrad = dot_nt(w[2].reshape(NY * BLK, D), chunk(1, k))
        act[0, k] = (hgrad * gs[0, k]).astype(BF16)
        act[1, k] = (hgrad * gs[1, k]).astype(BF16)

    tokens_in(2, 0, None)
    tokens_in(2, 1, None)
    wait(w.at[0, pl.ds(0, NY - 1)], r_wy.at[0])
    wait(w.at[1, pl.ds(0, NY - 1)], r_wy.at[1])
    for k in (0, 1, 3, 2):
        forward(k)
    for k in (0, 1, 3, 2):
        wait(ks.at[1, 0], r_tokc.at[k, 1])

    def gradient(m):
        total = None
        for k in range(NX):
            term = dot_nn(act[m, k], chunk(1 if m == 2 else 0, k))
            total = term if total is None else total + term
        rys[m] = total.astype(BF16).reshape(NY, BLK, D)
        spread(
            rys.at[m, (y + 1) % NY], rys.at[m, (y + 2) % NY], rys.at[m, (y + 3) % NY], ryv.at[m], ryr.at[m],
            s_ry, r_ryv.at[m], r_ry.at[m], ys[1], ys[3],
        )

    wait(w.at[2, pl.ds(0, NY - 1)], r_wy.at[2])
    for k in (0, 1, 3, 2):
        backward(k)
    order = (0, 1, 2)
    for m in order:
        gradient(m)
    for m in order:
        hand_on(
            rys.at[m, (y + 1) % NY], rys.at[m, (y + 3) % NY], ryv.at[m], rym.at[m], ryr.at[m],
            s_ry, r_ryv.at[m], r_ry.at[m], ys[1], ys[3],
        )

    above, below = (y + NY - 1) % NY, (y + 1) % NY
    wait(qn.at[1, above], r_q.at[1, 0])
    send(qn.at[1, above, :, first], qn.at[1, above, :, first], s_q, r_q.at[1, 1], ys[1])
    wait(qn.at[1, below], r_q.at[1, 2])
    send(qn.at[1, below, :, second], qn.at[1, below, :, second], s_q, r_q.at[1, 1], ys[3])

    unp[:, :, BLK:, :] = jnp.zeros((3, 6, 8, 128), F32)
    for m in order:
        wait(ryr.at[m], r_ry.at[m])
        total = rys[m, y].astype(F32)
        total = total + ryr[m, 0].astype(F32) + ryr[m, 1].astype(F32)
        for j in range(6):
            unp[m, j, :BLK, :] = total[:, j * 128 : (j + 1) * 128]
        for zz in range(NZ):
            rzs[m, zz] = unp[m, :, zz * ROWS : zz * ROWS + 8, :].reshape(PACK, 128).astype(BF16)
        for k in far_first_z:
            send(rzs.at[m, (z + k) % NZ], rzr.at[m, k - 1], s_rz, r_rz.at[m], zs[k])

    for k in (2, 1, 3):
        send(qn.at[0, x], qn.at[0, x], s_q, r_q.at[0, k - 1], xs[k])

    for m in order:
        wait(rzr.at[m], r_rz.at[m])
        grad = rzs[m, z].astype(F32)
        for k in range(NZ - 1):
            grad = grad + rzr[m, k].astype(F32)
        old = wpk[m].reshape(6, 8, 128)
        stepped = old - grad.reshape(6, 8, 128)
        old_ms = jnp.sum(jnp.sum(old * old, axis=0), axis=-1, keepdims=True) * (1.0 / D)
        new_ms = jnp.sum(jnp.sum(stepped * stepped, axis=0), axis=-1, keepdims=True) * (1.0 / D)
        upd = stepped * jnp.sqrt(old_ms + EPS)[None] / jnp.sqrt(new_ms + EPS)[None]
        az1[m, z] = upd.reshape(PACK, 128).astype(BF16)
        for k in far_first_z:
            send(az1.at[m, z], az1.at[m, z], s_az, r_az.at[m], zs[k])

    for m in order:
        wait(az1.at[m, pl.ds(0, NZ - 1)], r_az.at[m])
        def put_new(j, v, m=m):
            wu[m, c, pos[0], :, j * 128 : (j + 1) * 128] = v
        unpack(m, az1, put_new)
        for k in (2, 1, 3):
            send(wu.at[m, c, pos[0]], wu.at[m, c, pos[0]], s_ay, r_ay.at[m], lines[0][k])

    def project(m, half, core):
        gu[m, half] = dot_nt(qn[core].reshape(NX * TOK, D), wu[m, core].reshape(NY * BLK, D))

    def query_hidden(half):
        gate = gu[0, half]
        hid_q[half] = (gate * jax.nn.sigmoid(gate) * gu[1, half]).astype(BF16).reshape(NX, TOK, NY * BLK)

    def partial_outputs(half, core):
        down = wu[2, core].reshape(NY * BLK, D)
        for k in (2, 1, 3):
            ps[half, k - 1] = dot_nn(hid_q[half, (pos[1 - half] + k) % NX], down).astype(BF16)
        spread(
            ps.at[half, 0], ps.at[half, 1], ps.at[half, 2], pv.at[half], pr.at[half],
            s_p, r_pv.at[half], r_p.at[half], lines[1 - half][1], lines[1 - half][3],
        )
        att[...] += dot_nn(hid_q[half, pos[1 - half]], down)

    for k in range(NX - 1):
        wait(qn.at[0, 0], r_q.at[0, k])
    wait(qn.at[1, 0], r_q.at[1, 1])
    for m in order:
        if m == 2:
            query_hidden(0)
            wait(wu.at[0, 1 - c], r_ac.at[0])
            project(0, 1, 1 - c)
        wait(wu.at[m, c, pl.ds(0, NY - 1)], r_ay.at[m])
        send(wu.at[m, c], wu.at[m, c], s_ac, r_ac.at[m], other)
        if m < 2:
            project(m, 0, c)
    partial_outputs(0, c)
    wait(wu.at[1, 1 - c], r_ac.at[1])
    project(1, 1, 1 - c)
    query_hidden(1)
    wait(wu.at[2, 1 - c], r_ac.at[2])
    partial_outputs(1, 1 - c)
    for half in range(2):
        hand_on(
            ps.at[half, 0], ps.at[half, 2], pv.at[half], pm.at[half], pr.at[half],
            s_p, r_pv.at[half], r_p.at[half], lines[1 - half][1], lines[1 - half][3],
        )

    wait(az0.at[:, pl.ds(0, NZ - 1)], s_az0)
    for _ in range(7):
        wait(ks.at[:, 0], s_tok)
    wait(w.at[:, pl.ds(0, NY - 1)], s_wy)
    wait(qn.at[:, pl.ds(0, NX - 1)], s_q)
    wait(rys.at[:, pl.ds(0, NY - 1)], s_ry)
    wait(rzr, s_rz)
    wait(az1.at[:, pl.ds(0, NZ - 1)], s_az)
    wait(wu.at[:, 0, pl.ds(0, NY - 1)], s_ay)
    wait(wu.at[:, 0], s_ac)
    wait(ps, s_p)

    result = att[...]
    for half in range(2):
        wait(pr.at[half], r_p.at[half])
        result = result + pr[half, 0].astype(F32) + pr[half, 1].astype(F32)
    out_ref[...] = result.astype(BF16)


def body(key_tokens, value_tokens, queries, token_rate, fast_weights):
    vmem = pltpu.VMEM
    dma = pltpu.SemaphoreType.DMA
    return pl.pallas_call(
        kernel,
        name="ttt_layer",
        out_shape=jax.ShapeDtypeStruct((TOK, D), BF16),
        in_specs=[pl.BlockSpec(memory_space=pl.ANY)] * 5,
        out_specs=pl.BlockSpec(memory_space=pltpu.VMEM),
        scratch_shapes=[
            vmem((TOK, D), BF16),
            vmem((TOK, D), BF16),
            vmem((TOK, D), BF16),
            vmem((1, TOK), F32),
            vmem((3, ROWS, D), BF16),
            vmem((3, PACK, 128), F32),
            vmem((3, NZ, PACK, 128), BF16),
            vmem((3, NY, BLK, D), BF16),
            vmem((2, 2 * NX, TOK, D), BF16),
            vmem((2, NX, TOK, D), BF16),
            vmem((2, NX, NY * BLK, 2 * TOK), F32),
            vmem((3, NX, NY * BLK, 2 * TOK), BF16),
            vmem((3, NY, BLK, D), BF16),
            vmem((3, 2, BLK, HALF), BF16),
            vmem((3, 2, BLK, HALF), BF16),
            vmem((3, 2, BLK, D), BF16),
            vmem((3, NZ, PACK, 128), BF16),
            vmem((3, NZ - 1, PACK, 128), BF16),
            vmem((3, NZ, PACK, 128), BF16),
            vmem((3, 2, NY, BLK, D), BF16),
            vmem((3, 6, BLK + 8, 128), F32),
            vmem((2, 2, NX * TOK, NY * BLK), F32),
            vmem((2, NX, TOK, NY * BLK), BF16),
            vmem((2, NX - 1, TOK, D), BF16),
            vmem((2, 2, TOK, HALF), BF16),
            vmem((2, 2, TOK, HALF), BF16),
            vmem((2, 2, TOK, D), BF16),
            vmem((TOK, D), F32),
            dma((5,)), dma, dma((3,)), dma, dma((3,)), dma, dma((3, 2)), dma((NX, 2)), dma, dma((2, 3)),
            dma, dma((3, 2)), dma((3,)), dma, dma((3,)), dma, dma((3,)), dma, dma((3,)), dma, dma((3,)),
            dma, dma((2, 2)), dma((2,)),
        ],
        compiler_params=pltpu.CompilerParams(
            collective_id=0, has_side_effects=True, vmem_limit_bytes=56250000
        ),
    )(key_tokens, value_tokens, queries, token_rate.reshape(1, TOK), fast_weights)


def solution(mesh):
    rows = P(("grp", "dev"), None)
    in_specs = (rows, rows, rows, P(("grp", "dev")), P(None, ("grp", "dev"), None))
    return jax.shard_map(body, mesh=mesh, in_specs=in_specs, out_specs=rows, check_vma=False)
```

```python
import functools

import jax
import jax.numpy as jnp
from jax import lax
from jax.experimental import pallas as pl
from jax.experimental.pallas import tpu as pltpu
from jax.sharding import PartitionSpec as P

D = 768
TOK = 128
EPS = 1e-06
NX, NY, NZ = 4, 4, 8
ROWS = 6
BLK = NZ * ROWS
PACK = 48
HALF = D // 2
MESH = pl.DeviceIdType.MESH
F32 = jnp.float32
BF16 = jnp.bfloat16


def dot_nt(a, b):
    return lax.dot_general(a, b, (((1,), (1,)), ((), ())), preferred_element_type=F32)


def dot_nn(a, b):
    return lax.dot_general(a, b, (((1,), (0,)), ((), ())), preferred_element_type=F32)


def device(x, y, z, c):
    return ((z // 4) * 2 + c, (z % 4) * 16 + y * 4 + x)


def rms_scale(rows):
    return lax.rsqrt(jnp.mean(rows * rows, axis=-1, keepdims=True) + EPS)


def kernel(
    key_hbm, val_hbm, qry_hbm, rate_hbm, w_hbm, out_ref,
    key_ref, val_ref, qry_ref, rate_ref, w_ref,
    wpk, az0, w, ks, qn, gs, act, rys, ryv, rym, ryr, rzs, rzr, az1, wu, unp, gu, hid_q, ps, pv, pm, pr, att,
    s_in, s_az0, r_az0, s_wy, r_wy, s_tok, r_tok, r_tokc, s_q, r_q,
    s_ry, r_ryv, r_ry, s_rz, r_rz, s_az, r_az, s_ay, r_ay, s_ac, r_ac, s_p, r_pv, r_p,
):
    g = lax.axis_index("grp")
    d = lax.axis_index("dev")
    x, y, z, c = d % 4, (d // 4) % 4, (g // 2) * 4 + d // 16, g % 2
    other = device(x, y, z, 1 - c)
    xs = [device((x + k) % NX, y, z, c) for k in range(NX)]
    ys = [device(x, (y + k) % NY, z, c) for k in range(NY)]
    zs = [device(x, y, (z + k) % NZ, c) for k in range(NZ)]
    pos = (y * (1 - c) + x * c, x * (1 - c) + y * c)
    lines = (
        [device((x + k * c) % NX, (y + k * (1 - c)) % NY, z, c) for k in range(NX)],
        [device((x + k * (1 - c)) % NX, (y + k * c) % NY, z, c) for k in range(NX)],
    )
    far_first_z = (4, 3, 5, 2, 6, 1, 7)

    barrier = pltpu.get_barrier_semaphore()
    peers = [zs[k] for k in far_first_z] + [ys[2], xs[2], ys[1], ys[3], xs[1], xs[3], other]
    for peer in peers:
        pl.semaphore_signal(barrier, inc=1, device_id=peer, device_id_type=MESH)

    fetches = [
        pltpu.make_async_copy(src, dst, s_in.at[i])
        for i, (src, dst) in enumerate(
            [(w_hbm, w_ref), (key_hbm, key_ref), (val_hbm, val_ref), (rate_hbm, rate_ref), (qry_hbm, qry_ref)]
        )
    ]
    for fetch in fetches:
        fetch.start()

    def send(src, dst, ssem, rsem, peer):
        pltpu.make_async_remote_copy(
            src_ref=src, dst_ref=dst, send_sem=ssem, recv_sem=rsem, device_id=peer, device_id_type=MESH
        ).start()

    def wait(ref, sem):
        pltpu.make_async_copy(ref, ref, sem).wait()

    first, second = pl.ds(0, HALF), pl.ds(HALF, HALF)

    def spread(right1, far, left1, via, got, ssem, via_sem, got_sem, right, left):
        send(far.at[:, first], via.at[0], ssem, via_sem.at[0], right)
        send(far.at[:, second], via.at[1], ssem, via_sem.at[1], left)
        send(right1.at[:, second], got.at[0, :, second], ssem, got_sem, right)
        send(left1.at[:, first], got.at[1, :, first], ssem, got_sem, left)

    def hand_on(right1, left1, via, summed, got, ssem, via_sem, got_sem, right, left):
        wait(via.at[0], via_sem.at[0])
        summed[0] = (right1[:, :HALF].astype(F32) + via[0].astype(F32)).astype(BF16)
        send(summed.at[0], got.at[0, :, first], ssem, got_sem, right)
        wait(via.at[1], via_sem.at[1])
        summed[1] = (left1[:, HALF:].astype(F32) + via[1].astype(F32)).astype(BF16)
        send(summed.at[1], got.at[1, :, second], ssem, got_sem, left)

    wpk[...] = jnp.zeros_like(wpk)
    fetches[0].wait()
    for m in range(3):
        rows = w_ref[m].astype(F32)
        for j in range(6):
            wpk[m, j * 8 : j * 8 + ROWS, :] = rows[:, j * 128 : (j + 1) * 128]
        az0[m, z] = wpk[m].astype(BF16)

    slot = x * 2 + c
    fetches[1].wait()
    keys = key_ref[...].astype(F32)
    ks[0, slot] = (keys * rms_scale(keys)).astype(BF16)
    fetches[2].wait()
    fetches[3].wait()
    diagonal = lax.broadcasted_iota(jnp.int32, (TOK, TOK), 0) == lax.broadcasted_iota(jnp.int32, (TOK, TOK), 1)
    rate = jnp.sum(jnp.where(diagonal, rate_ref[...], 0.0), axis=-1, keepdims=True)
    ks[1, slot] = (-(rate * val_ref[...].astype(F32))).astype(BF16)

    fetches[4].wait()
    queries = qry_ref[...].astype(F32)
    normed = (queries * rms_scale(queries)).astype(BF16)
    qn[0, x] = normed
    qn[1, y] = normed

    pl.semaphore_wait(barrier, len(peers))

    def send_tok(kind, sl, sem, peer):
        send(ks.at[kind, sl], ks.at[kind, sl], s_tok, sem, peer)
    for k in far_first_z:
        send(az0.at[0, z], az0.at[0, z], s_az0, r_az0.at[0], zs[k])
    send_tok(0, slot, r_tok.at[0, 0], xs[1])
    send_tok(1, slot, r_tok.at[2, 1], xs[3])
    send_tok(1, slot, r_tok.at[0, 1], xs[1])
    send_tok(0, slot, r_tok.at[2, 0], xs[3])
    for kind in range(2):
        send_tok(kind, slot, r_tokc.at[0, kind], other)
    for k in (1, 3):
        send(qn.at[1, y], qn.at[1, y], s_q, r_q.at[1, k - 1], ys[k])
    for m in (1, 2):
        for k in far_first_z:
            send(az0.at[m, z], az0.at[m, z], s_az0, r_az0.at[m], zs[k])

    def token_slot(k, core):
        return ((x + NX - k) % NX) * 2 + core

    def tokens_in(k, kind, onward):
        sl = token_slot(k, c)
        wait(ks.at[kind, sl], r_tok.at[k - 1, kind])
        if onward is not None:
            send_tok(kind, sl, r_tok.at[1, kind], onward)
        send_tok(kind, sl, r_tokc.at[k, kind], other)

    def unpack(m, packed, store):
        for zz in range(NZ):
            unp[m, :, zz * ROWS : zz * ROWS + 8, :] = packed[m, zz].astype(F32).reshape(6, 8, 128)
        for j in range(6):
            store(j, unp[m, j, :BLK, :].astype(BF16))

    def old_weights(m):
        wait(az0.at[m, pl.ds(0, NZ - 1)], r_az0.at[m])
        def put(j, v):
            w[m, y, :, j * 128 : (j + 1) * 128] = v
        unpack(m, az0, put)
        for k in (2, 1, 3):
            send(w.at[m, y], w.at[m, y], s_wy, r_wy.at[m], ys[k])

    old_weights(0)
    old_weights(1)
    tokens_in(1, 0, xs[1])
    tokens_in(3, 1, xs[3])
    old_weights(2)

    lane = lax.broadcasted_iota(jnp.int32, (TOK, 128), 1)
    for p in range(6):
        cols = slice(p * 128, (p + 1) * 128)
        qp, kp, vp = qry_ref[:, cols], key_ref[:, cols], val_ref[:, cols]
        zero = jnp.zeros_like(qp)
        both = jnp.concatenate([jnp.where(lane < 64, qp, zero), jnp.where(lane < 64, zero, qp)], axis=0)
        scores = dot_nt(both, kp) * 0.125
        e = jnp.exp(scores - jnp.max(scores, axis=-1, keepdims=True))
        probs = (e / jnp.sum(e, axis=-1, keepdims=True)).astype(BF16)
        mixed = dot_nn(probs, vp)
        att[:, cols] = jnp.where(lane < 64, mixed[:TOK], mixed[TOK:])

    tokens_in(1, 1, None)
    tokens_in(3, 0, None)

    def chunk(kind, k):
        xx = (x + NX - k) % NX
        return ks[kind, pl.ds(xx * 2, 2)].reshape(2 * TOK, D)

    def forward(k):
        wait(ks.at[0, 0], r_tokc.at[k, 0])
        kn = chunk(0, k)
        gate = dot_nt(w[0].reshape(NY * BLK, D), kn)
        up = dot_nt(w[1].reshape(NY * BLK, D), kn)
        sig = jax.nn.sigmoid(gate)
        silu = gate * sig
        act[2, k] = (silu * up).astype(BF16)
        gs[0, k] = up * sig * (1.0 + gate * (1.0 - sig))
        gs[1, k] = silu

    def backward(k):
        hgrad = dot_nt(w[2].reshape(NY * BLK, D), chunk(1, k))
        act[0, k] = (hgrad * gs[0, k]).astype(BF16)
        act[1, k] = (hgrad * gs[1, k]).astype(BF16)

    tokens_in(2, 0, None)
    tokens_in(2, 1, None)
    wait(w.at[0, pl.ds(0, NY - 1)], r_wy.at[0])
    wait(w.at[1, pl.ds(0, NY - 1)], r_wy.at[1])
    for k in (0, 1, 3, 2):
        forward(k)
    for k in (0, 1, 3, 2):
        wait(ks.at[1, 0], r_tokc.at[k, 1])

    def gradient(m):
        total = None
        for k in range(NX):
            term = dot_nn(act[m, k], chunk(1 if m == 2 else 0, k))
            total = term if total is None else total + term
        rys[m] = total.astype(BF16).reshape(NY, BLK, D)
        spread(
            rys.at[m, (y + 1) % NY], rys.at[m, (y + 2) % NY], rys.at[m, (y + 3) % NY], ryv.at[m], ryr.at[m],
            s_ry, r_ryv.at[m], r_ry.at[m], ys[1], ys[3],
        )

    wait(w.at[2, pl.ds(0, NY - 1)], r_wy.at[2])
    for k in (0, 1, 3, 2):
        backward(k)
    order = (0, 1, 2)
    for m in order:
        gradient(m)
    for m in order:
        hand_on(
            rys.at[m, (y + 1) % NY], rys.at[m, (y + 3) % NY], ryv.at[m], rym.at[m], ryr.at[m],
            s_ry, r_ryv.at[m], r_ry.at[m], ys[1], ys[3],
        )

    above, below = (y + NY - 1) % NY, (y + 1) % NY
    wait(qn.at[1, above], r_q.at[1, 0])
    send(qn.at[1, above, :, first], qn.at[1, above, :, first], s_q, r_q.at[1, 1], ys[1])
    wait(qn.at[1, below], r_q.at[1, 2])
    send(qn.at[1, below, :, second], qn.at[1, below, :, second], s_q, r_q.at[1, 1], ys[3])

    unp[:, :, BLK:, :] = jnp.zeros((3, 6, 8, 128), F32)
    for m in order:
        wait(ryr.at[m], r_ry.at[m])
        total = rys[m, y].astype(F32)
        total = total + ryr[m, 0].astype(F32) + ryr[m, 1].astype(F32)
        for j in range(6):
            unp[m, j, :BLK, :] = total[:, j * 128 : (j + 1) * 128]
        for zz in range(NZ):
            rzs[m, zz] = unp[m, :, zz * ROWS : zz * ROWS + 8, :].reshape(PACK, 128).astype(BF16)
        for k in far_first_z:
            send(rzs.at[m, (z + k) % NZ], rzr.at[m, k - 1], s_rz, r_rz.at[m], zs[k])

    for k in (2, 1, 3):
        send(qn.at[0, x], qn.at[0, x], s_q, r_q.at[0, k - 1], xs[k])

    for m in order:
        wait(rzr.at[m], r_rz.at[m])
        grad = rzs[m, z].astype(F32)
        for k in range(NZ - 1):
            grad = grad + rzr[m, k].astype(F32)
        old = wpk[m].reshape(6, 8, 128)
        stepped = old - grad.reshape(6, 8, 128)
        old_ms = jnp.sum(jnp.sum(old * old, axis=0), axis=-1, keepdims=True) * (1.0 / D)
        new_ms = jnp.sum(jnp.sum(stepped * stepped, axis=0), axis=-1, keepdims=True) * (1.0 / D)
        upd = stepped * jnp.sqrt(old_ms + EPS)[None] / jnp.sqrt(new_ms + EPS)[None]
        az1[m, z] = upd.reshape(PACK, 128).astype(BF16)
        for k in far_first_z:
            send(az1.at[m, z], az1.at[m, z], s_az, r_az.at[m], zs[k])

    for m in order:
        wait(az1.at[m, pl.ds(0, NZ - 1)], r_az.at[m])
        def put_new(j, v, m=m):
            wu[m, c, pos[0], :, j * 128 : (j + 1) * 128] = v
        unpack(m, az1, put_new)
        for k in (2, 1, 3):
            send(wu.at[m, c, pos[0]], wu.at[m, c, pos[0]], s_ay, r_ay.at[m], lines[0][k])

    def project(m, half, core):
        gu[m, half] = dot_nt(qn[core].reshape(NX * TOK, D), wu[m, core].reshape(NY * BLK, D))

    def query_hidden(half):
        gate = gu[0, half]
        hid_q[half] = (gate * jax.nn.sigmoid(gate) * gu[1, half]).astype(BF16).reshape(NX, TOK, NY * BLK)

    def partial_outputs(half, core):
        down = wu[2, core].reshape(NY * BLK, D)
        for k in (2, 1, 3):
            ps[half, k - 1] = dot_nn(hid_q[half, (pos[1 - half] + k) % NX], down).astype(BF16)
        spread(
            ps.at[half, 0], ps.at[half, 1], ps.at[half, 2], pv.at[half], pr.at[half],
            s_p, r_pv.at[half], r_p.at[half], lines[1 - half][1], lines[1 - half][3],
        )
        att[...] += dot_nn(hid_q[half, pos[1 - half]], down)

    for k in range(NX - 1):
        wait(qn.at[0, 0], r_q.at[0, k])
    wait(qn.at[1, 0], r_q.at[1, 1])
    for m in order:
        if m == 2:
            query_hidden(0)
            wait(wu.at[0, 1 - c], r_ac.at[0])
            project(0, 1, 1 - c)
        wait(wu.at[m, c, pl.ds(0, NY - 1)], r_ay.at[m])
        send(wu.at[m, c], wu.at[m, c], s_ac, r_ac.at[m], other)
        if m < 2:
            project(m, 0, c)
    partial_outputs(0, c)
    wait(wu.at[1, 1 - c], r_ac.at[1])
    project(1, 1, 1 - c)
    query_hidden(1)
    wait(wu.at[2, 1 - c], r_ac.at[2])
    partial_outputs(1, 1 - c)
    for half in range(2):
        hand_on(
            ps.at[half, 0], ps.at[half, 2], pv.at[half], pm.at[half], pr.at[half],
            s_p, r_pv.at[half], r_p.at[half], lines[1 - half][1], lines[1 - half][3],
        )

    wait(az0.at[:, pl.ds(0, NZ - 1)], s_az0)
    for _ in range(7):
        wait(ks.at[:, 0], s_tok)
    wait(w.at[:, pl.ds(0, NY - 1)], s_wy)
    wait(qn.at[:, pl.ds(0, NX - 1)], s_q)
    wait(rys.at[:, pl.ds(0, NY - 1)], s_ry)
    wait(rzr, s_rz)
    wait(az1.at[:, pl.ds(0, NZ - 1)], s_az)
    wait(wu.at[:, 0, pl.ds(0, NY - 1)], s_ay)
    wait(wu.at[:, 0], s_ac)
    wait(ps, s_p)

    result = att[...]
    for half in range(2):
        wait(pr.at[half], r_p.at[half])
        result = result + pr[half, 0].astype(F32) + pr[half, 1].astype(F32)
    out_ref[...] = result.astype(BF16)


def body(key_tokens, value_tokens, queries, token_rate, fast_weights):
    vmem = pltpu.VMEM
    dma = pltpu.SemaphoreType.DMA
    return pl.pallas_call(
        kernel,
        name="ttt_layer",
        out_shape=jax.ShapeDtypeStruct((TOK, D), BF16),
        in_specs=[pl.BlockSpec(memory_space=pl.ANY)] * 5,
        out_specs=pl.BlockSpec(memory_space=pltpu.VMEM),
        scratch_shapes=[
            vmem((TOK, D), BF16),
            vmem((TOK, D), BF16),
            vmem((TOK, D), BF16),
            vmem((1, TOK), F32),
            vmem((3, ROWS, D), BF16),
            vmem((3, PACK, 128), F32),
            vmem((3, NZ, PACK, 128), BF16),
            vmem((3, NY, BLK, D), BF16),
            vmem((2, 2 * NX, TOK, D), BF16),
            vmem((2, NX, TOK, D), BF16),
            vmem((2, NX, NY * BLK, 2 * TOK), F32),
            vmem((3, NX, NY * BLK, 2 * TOK), BF16),
            vmem((3, NY, BLK, D), BF16),
            vmem((3, 2, BLK, HALF), BF16),
            vmem((3, 2, BLK, HALF), BF16),
            vmem((3, 2, BLK, D), BF16),
            vmem((3, NZ, PACK, 128), BF16),
            vmem((3, NZ - 1, PACK, 128), BF16),
            vmem((3, NZ, PACK, 128), BF16),
            vmem((3, 2, NY, BLK, D), BF16),
            vmem((3, 6, BLK + 8, 128), F32),
            vmem((2, 2, NX * TOK, NY * BLK), F32),
            vmem((2, NX, TOK, NY * BLK), BF16),
            vmem((2, NX - 1, TOK, D), BF16),
            vmem((2, 2, TOK, HALF), BF16),
            vmem((2, 2, TOK, HALF), BF16),
            vmem((2, 2, TOK, D), BF16),
            vmem((TOK, D), F32),
            dma((5,)), dma, dma((3,)), dma, dma((3,)), dma, dma((3, 2)), dma((NX, 2)), dma, dma((2, 3)),
            dma, dma((3, 2)), dma((3,)), dma, dma((3,)), dma, dma((3,)), dma, dma((3,)), dma, dma((3,)),
            dma, dma((2, 2)), dma((2,)),
        ],
        compiler_params=pltpu.CompilerParams(
            collective_id=0, has_side_effects=True, vmem_limit_bytes=56 << 20
        ),
    )(key_tokens, value_tokens, queries, token_rate.reshape(1, TOK), fast_weights)


def solution(mesh):
    rows = P(("grp", "dev"), None)
    in_specs = (rows, rows, rows, P(("grp", "dev")), P(None, ("grp", "dev"), None))
    return jax.shard_map(body, mesh=mesh, in_specs=in_specs, out_specs=rows, check_vma=False)
```

```python
import functools

import jax
import jax.numpy as jnp
from jax import lax
from jax.experimental import pallas as pl
from jax.experimental.pallas import tpu as pltpu
from jax.sharding import PartitionSpec as P

D = 768
TOK = 128
EPS = 1e-06
NX, NY, NZ = 4, 4, 8
ROWS = 6
BLK = NZ * ROWS
PACK = 48
HALF = D // 2
MESH = pl.DeviceIdType.MESH
F32 = jnp.float32
BF16 = jnp.bfloat16


def dot_nt(a, b):
    return lax.dot_general(a, b, (((1,), (1,)), ((), ())), preferred_element_type=F32)


def dot_nn(a, b):
    return lax.dot_general(a, b, (((1,), (0,)), ((), ())), preferred_element_type=F32)


def device(x, y, z, c):
    return ((z // 4) * 2 + c, (z % 4) * 16 + y * 4 + x)


def rms_scale(rows):
    return lax.rsqrt(jnp.mean(rows * rows, axis=-1, keepdims=True) + EPS)


def kernel(
    key_hbm, val_hbm, qry_hbm, rate_hbm, w_hbm, out_ref,
    key_ref, val_ref, qry_ref, rate_ref, w_ref,
    wpk, az0, w, ks, qn, gs, act, rys, ryv, rym, ryr, rzs, rzr, az1, wu, unp, gu, hid_q, ps, pv, pm, pr, att, held,
    s_in, s_az0, r_az0, s_wy, r_wy, s_tok, r_tok, r_tokc, s_q, r_q,
    s_ry, r_ryv, r_ry, s_rz, r_rz, s_az, r_az, s_ay, r_ay, s_ac, r_ac, s_p, r_pv, r_p, s_out,
):
    g = lax.axis_index("grp")
    d = lax.axis_index("dev")
    x, y, z, c = d % 4, (d // 4) % 4, (g // 2) * 4 + d // 16, g % 2
    other = device(x, y, z, 1 - c)
    xs = [device((x + k) % NX, y, z, c) for k in range(NX)]
    ys = [device(x, (y + k) % NY, z, c) for k in range(NY)]
    zs = [device(x, y, (z + k) % NZ, c) for k in range(NZ)]
    pos = (y * (1 - c) + x * c, x * (1 - c) + y * c)
    lines = (
        [device((x + k * c) % NX, (y + k * (1 - c)) % NY, z, c) for k in range(NX)],
        [device((x + k * (1 - c)) % NX, (y + k * c) % NY, z, c) for k in range(NX)],
    )
    far_first_z = (4, 3, 5, 2, 6, 1, 7)

    barrier = pltpu.get_barrier_semaphore()
    peers = [zs[k] for k in far_first_z] + [ys[2], xs[2], ys[1], ys[3], xs[1], xs[3], other]
    for peer in peers:
        pl.semaphore_signal(barrier, inc=1, device_id=peer, device_id_type=MESH)

    fetches = [
        pltpu.make_async_copy(src, dst, s_in.at[i])
        for i, (src, dst) in enumerate(
            [(w_hbm, w_ref), (key_hbm, key_ref), (val_hbm, val_ref), (rate_hbm, rate_ref), (qry_hbm, qry_ref)]
        )
    ]
    for fetch in fetches:
        fetch.start()

    def send(src, dst, ssem, rsem, peer):
        pltpu.make_async_remote_copy(
            src_ref=src, dst_ref=dst, send_sem=ssem, recv_sem=rsem, device_id=peer, device_id_type=MESH
        ).start()

    def wait(ref, sem):
        pltpu.make_async_copy(ref, ref, sem).wait()

    first, second = pl.ds(0, HALF), pl.ds(HALF, HALF)

    def spread(right1, far, left1, via, got, ssem, via_sem, got_sem, right, left):
        send(far.at[:, first], via.at[0], ssem, via_sem.at[0], right)
        send(far.at[:, second], via.at[1], ssem, via_sem.at[1], left)
        send(right1.at[:, second], got.at[0, :, second], ssem, got_sem, right)
        send(left1.at[:, first], got.at[1, :, first], ssem, got_sem, left)

    def hand_on(right1, left1, via, summed, got, ssem, via_sem, got_sem, right, left):
        wait(via.at[0], via_sem.at[0])
        summed[0] = (right1[:, :HALF].astype(F32) + via[0].astype(F32)).astype(BF16)
        send(summed.at[0], got.at[0, :, first], ssem, got_sem, right)
        wait(via.at[1], via_sem.at[1])
        summed[1] = (left1[:, HALF:].astype(F32) + via[1].astype(F32)).astype(BF16)
        send(summed.at[1], got.at[1, :, second], ssem, got_sem, left)

    wpk[...] = jnp.zeros_like(wpk)
    fetches[0].wait()
    for m in range(3):
        rows = w_ref[m].astype(F32)
        for j in range(6):
            wpk[m, j * 8 : j * 8 + ROWS, :] = rows[:, j * 128 : (j + 1) * 128]
        az0[m, z] = wpk[m].astype(BF16)

    slot = x * 2 + c
    fetches[1].wait()
    keys = key_ref[...].astype(F32)
    ks[0, slot] = (keys * rms_scale(keys)).astype(BF16)
    fetches[2].wait()
    fetches[3].wait()
    diagonal = lax.broadcasted_iota(jnp.int32, (TOK, TOK), 0) == lax.broadcasted_iota(jnp.int32, (TOK, TOK), 1)
    rate = jnp.sum(jnp.where(diagonal, rate_ref[...], 0.0), axis=-1, keepdims=True)
    ks[1, slot] = (-(rate * val_ref[...].astype(F32))).astype(BF16)

    fetches[4].wait()
    queries = qry_ref[...].astype(F32)
    normed = (queries * rms_scale(queries)).astype(BF16)
    qn[0, x] = normed
    qn[1, y] = normed

    pl.semaphore_wait(barrier, len(peers))

    def send_tok(kind, sl, sem, peer):
        send(ks.at[kind, sl], ks.at[kind, sl], s_tok, sem, peer)
    for k in far_first_z:
        send(az0.at[0, z], az0.at[0, z], s_az0, r_az0.at[0], zs[k])
    send_tok(0, slot, r_tok.at[0, 0], xs[1])
    send_tok(1, slot, r_tok.at[2, 1], xs[3])
    send_tok(1, slot, r_tok.at[0, 1], xs[1])
    send_tok(0, slot, r_tok.at[2, 0], xs[3])
    for kind in range(2):
        send_tok(kind, slot, r_tokc.at[0, kind], other)
    for k in (1, 3):
        send(qn.at[1, y], qn.at[1, y], s_q, r_q.at[1, k - 1], ys[k])
    for m in (1, 2):
        for k in far_first_z:
            send(az0.at[m, z], az0.at[m, z], s_az0, r_az0.at[m], zs[k])

    def token_slot(k, core):
        return ((x + NX - k) % NX) * 2 + core

    def tokens_in(k, kind, onward):
        sl = token_slot(k, c)
        wait(ks.at[kind, sl], r_tok.at[k - 1, kind])
        if onward is not None:
            send_tok(kind, sl, r_tok.at[1, kind], onward)
        send_tok(kind, sl, r_tokc.at[k, kind], other)

    def unpack(m, packed, store):
        for zz in range(NZ):
            unp[m, :, zz * ROWS : zz * ROWS + 8, :] = packed[m, zz].astype(F32).reshape(6, 8, 128)
        for j in range(6):
            store(j, unp[m, j, :BLK, :].astype(BF16))

    def old_weights(m):
        wait(az0.at[m, pl.ds(0, NZ - 1)], r_az0.at[m])
        def put(j, v):
            w[m, y, :, j * 128 : (j + 1) * 128] = v
        unpack(m, az0, put)
        for k in (2, 1, 3):
            send(w.at[m, y], w.at[m, y], s_wy, r_wy.at[m], ys[k])

    old_weights(0)
    old_weights(1)
    tokens_in(1, 0, xs[1])
    tokens_in(3, 1, xs[3])
    old_weights(2)

    lane = lax.broadcasted_iota(jnp.int32, (TOK, 128), 1)
    for p in range(6):
        cols = slice(p * 128, (p + 1) * 128)
        qp, kp, vp = qry_ref[:, cols], key_ref[:, cols], val_ref[:, cols]
        zero = jnp.zeros_like(qp)
        both = jnp.concatenate([jnp.where(lane < 64, qp, zero), jnp.where(lane < 64, zero, qp)], axis=0)
        scores = dot_nt(both, kp) * 0.125
        e = jnp.exp(scores - jnp.max(scores, axis=-1, keepdims=True))
        probs = (e / jnp.sum(e, axis=-1, keepdims=True)).astype(BF16)
        mixed = dot_nn(probs, vp)
        att[:, cols] = jnp.where(lane < 64, mixed[:TOK], mixed[TOK:])

    tokens_in(1, 1, None)
    tokens_in(3, 0, None)

    def chunk(kind, k):
        xx = (x + NX - k) % NX
        return ks[kind, pl.ds(xx * 2, 2)].reshape(2 * TOK, D)

    def forward(k):
        wait(ks.at[0, 0], r_tokc.at[k, 0])
        kn = chunk(0, k)
        gate = dot_nt(w[0].reshape(NY * BLK, D), kn)
        up = dot_nt(w[1].reshape(NY * BLK, D), kn)
        sig = jax.nn.sigmoid(gate)
        silu = gate * sig
        act[2, k] = (silu * up).astype(BF16)
        gs[0, k] = up * sig * (1.0 + gate * (1.0 - sig))
        gs[1, k] = silu

    def backward(k):
        hgrad = dot_nt(w[2].reshape(NY * BLK, D), chunk(1, k))
        act[0, k] = (hgrad * gs[0, k]).astype(BF16)
        act[1, k] = (hgrad * gs[1, k]).astype(BF16)

    tokens_in(2, 0, None)
    tokens_in(2, 1, None)
    wait(w.at[0, pl.ds(0, NY - 1)], r_wy.at[0])
    wait(w.at[1, pl.ds(0, NY - 1)], r_wy.at[1])
    for k in (0, 1, 3, 2):
        forward(k)
    for k in (0, 1, 3, 2):
        wait(ks.at[1, 0], r_tokc.at[k, 1])

    def gradient(m):
        total = None
        for k in range(NX):
            term = dot_nn(act[m, k], chunk(1 if m == 2 else 0, k))
            total = term if total is None else total + term
        rys[m] = total.astype(BF16).reshape(NY, BLK, D)
        spread(
            rys.at[m, (y + 1) % NY], rys.at[m, (y + 2) % NY], rys.at[m, (y + 3) % NY], ryv.at[m], ryr.at[m],
            s_ry, r_ryv.at[m], r_ry.at[m], ys[1], ys[3],
        )

    wait(w.at[2, pl.ds(0, NY - 1)], r_wy.at[2])
    for k in (0, 1, 3, 2):
        backward(k)
    order = (0, 1, 2)
    for m in order:
        gradient(m)
    for m in order:
        hand_on(
            rys.at[m, (y + 1) % NY], rys.at[m, (y + 3) % NY], ryv.at[m], rym.at[m], ryr.at[m],
            s_ry, r_ryv.at[m], r_ry.at[m], ys[1], ys[3],
        )

    above, below = (y + NY - 1) % NY, (y + 1) % NY
    wait(qn.at[1, above], r_q.at[1, 0])
    send(qn.at[1, above, :, first], qn.at[1, above, :, first], s_q, r_q.at[1, 1], ys[1])
    wait(qn.at[1, below], r_q.at[1, 2])
    send(qn.at[1, below, :, second], qn.at[1, below, :, second], s_q, r_q.at[1, 1], ys[3])

    unp[:, :, BLK:, :] = jnp.zeros((3, 6, 8, 128), F32)
    for m in order:
        wait(ryr.at[m], r_ry.at[m])
        total = rys[m, y].astype(F32)
        total = total + ryr[m, 0].astype(F32) + ryr[m, 1].astype(F32)
        for j in range(6):
            unp[m, j, :BLK, :] = total[:, j * 128 : (j + 1) * 128]
        for zz in range(NZ):
            rzs[m, zz] = unp[m, :, zz * ROWS : zz * ROWS + 8, :].reshape(PACK, 128).astype(BF16)
        for k in far_first_z:
            send(rzs.at[m, (z + k) % NZ], rzr.at[m, k - 1], s_rz, r_rz.at[m], zs[k])

    for k in (2, 1, 3):
        send(qn.at[0, x], qn.at[0, x], s_q, r_q.at[0, k - 1], xs[k])

    for m in order:
        wait(rzr.at[m], r_rz.at[m])
        grad = rzs[m, z].astype(F32)
        for k in range(NZ - 1):
            grad = grad + rzr[m, k].astype(F32)
        old = wpk[m].reshape(6, 8, 128)
        stepped = old - grad.reshape(6, 8, 128)
        old_ms = jnp.sum(jnp.sum(old * old, axis=0), axis=-1, keepdims=True) * (1.0 / D)
        new_ms = jnp.sum(jnp.sum(stepped * stepped, axis=0), axis=-1, keepdims=True) * (1.0 / D)
        upd = stepped * jnp.sqrt(old_ms + EPS)[None] / jnp.sqrt(new_ms + EPS)[None]
        az1[m, z] = upd.reshape(PACK, 128).astype(BF16)
        for k in far_first_z:
            send(az1.at[m, z], az1.at[m, z], s_az, r_az.at[m], zs[k])

    for m in order:
        wait(az1.at[m, pl.ds(0, NZ - 1)], r_az.at[m])
        def put_new(j, v, m=m):
            wu[m, c, pos[0], :, j * 128 : (j + 1) * 128] = v
        unpack(m, az1, put_new)
        for k in (2, 1, 3):
            send(wu.at[m, c, pos[0]], wu.at[m, c, pos[0]], s_ay, r_ay.at[m], lines[0][k])

    def project(m, half, core):
        gu[m, half] = dot_nt(qn[core].reshape(NX * TOK, D), wu[m, core].reshape(NY * BLK, D))

    def query_hidden(half):
        gate = gu[0, half]
        hid_q[half] = (gate * jax.nn.sigmoid(gate) * gu[1, half]).astype(BF16).reshape(NX, TOK, NY * BLK)

    def partial_outputs(half, core):
        down = wu[2, core].reshape(NY * BLK, D)
        for k in (2, 1, 3):
            ps[half, k - 1] = dot_nn(hid_q[half, (pos[1 - half] + k) % NX], down).astype(BF16)
        spread(
            ps.at[half, 0], ps.at[half, 1], ps.at[half, 2], pv.at[half], pr.at[half],
            s_p, r_pv.at[half], r_p.at[half], lines[1 - half][1], lines[1 - half][3],
        )
        att[...] += dot_nn(hid_q[half, pos[1 - half]], down)

    for k in range(NX - 1):
        wait(qn.at[0, 0], r_q.at[0, k])
    wait(qn.at[1, 0], r_q.at[1, 1])
    for m in order:
        if m == 2:
            query_hidden(0)
            wait(wu.at[0, 1 - c], r_ac.at[0])
            project(0, 1, 1 - c)
        wait(wu.at[m, c, pl.ds(0, NY - 1)], r_ay.at[m])
        send(wu.at[m, c], wu.at[m, c], s_ac, r_ac.at[m], other)
        if m < 2:
            project(m, 0, c)
    partial_outputs(0, c)
    wait(wu.at[1, 1 - c], r_ac.at[1])
    project(1, 1, 1 - c)
    query_hidden(1)
    wait(wu.at[2, 1 - c], r_ac.at[2])
    partial_outputs(1, 1 - c)
    for half in range(2):
        hand_on(
            ps.at[half, 0], ps.at[half, 2], pv.at[half], pm.at[half], pr.at[half],
            s_p, r_pv.at[half], r_p.at[half], lines[1 - half][1], lines[1 - half][3],
        )

    wait(az0.at[:, pl.ds(0, NZ - 1)], s_az0)
    for _ in range(7):
        wait(ks.at[:, 0], s_tok)
    wait(w.at[:, pl.ds(0, NY - 1)], s_wy)
    wait(qn.at[:, pl.ds(0, NX - 1)], s_q)
    wait(rys.at[:, pl.ds(0, NY - 1)], s_ry)
    wait(rzr, s_rz)
    wait(az1.at[:, pl.ds(0, NZ - 1)], s_az)
    wait(wu.at[:, 0, pl.ds(0, NY - 1)], s_ay)
    wait(wu.at[:, 0], s_ac)
    wait(ps, s_p)

    for half in range(2):
        wait(pr.at[half], r_p.at[half])
    writes = []
    for i in range(2):
        rows = slice(i * 64, (i + 1) * 64)
        result = att[rows, :]
        for half in range(2):
            result = result + pr[half, 0, rows, :].astype(F32) + pr[half, 1, rows, :].astype(F32)
        held[rows, :] = result.astype(BF16)
        part = pl.ds(i * 64, 64)
        writes.append(pltpu.make_async_copy(held.at[part], out_ref.at[part], s_out.at[i]))
        writes[i].start()
    for write in writes:
        write.wait()


def body(key_tokens, value_tokens, queries, token_rate, fast_weights):
    vmem = pltpu.VMEM
    dma = pltpu.SemaphoreType.DMA
    return pl.pallas_call(
        kernel,
        name="ttt_layer",
        out_shape=jax.ShapeDtypeStruct((TOK, D), BF16),
        in_specs=[pl.BlockSpec(memory_space=pl.ANY)] * 5,
        out_specs=pl.BlockSpec(memory_space=pl.ANY),
        scratch_shapes=[
            vmem((TOK, D), BF16),
            vmem((TOK, D), BF16),
            vmem((TOK, D), BF16),
            vmem((1, TOK), F32),
            vmem((3, ROWS, D), BF16),
            vmem((3, PACK, 128), F32),
            vmem((3, NZ, PACK, 128), BF16),
            vmem((3, NY, BLK, D), BF16),
            vmem((2, 2 * NX, TOK, D), BF16),
            vmem((2, NX, TOK, D), BF16),
            vmem((2, NX, NY * BLK, 2 * TOK), F32),
            vmem((3, NX, NY * BLK, 2 * TOK), BF16),
            vmem((3, NY, BLK, D), BF16),
            vmem((3, 2, BLK, HALF), BF16),
            vmem((3, 2, BLK, HALF), BF16),
            vmem((3, 2, BLK, D), BF16),
            vmem((3, NZ, PACK, 128), BF16),
            vmem((3, NZ - 1, PACK, 128), BF16),
            vmem((3, NZ, PACK, 128), BF16),
            vmem((3, 2, NY, BLK, D), BF16),
            vmem((3, 6, BLK + 8, 128), F32),
            vmem((2, 2, NX * TOK, NY * BLK), F32),
            vmem((2, NX, TOK, NY * BLK), BF16),
            vmem((2, NX - 1, TOK, D), BF16),
            vmem((2, 2, TOK, HALF), BF16),
            vmem((2, 2, TOK, HALF), BF16),
            vmem((2, 2, TOK, D), BF16),
            vmem((TOK, D), F32),
            vmem((TOK, D), BF16),
            dma((5,)), dma, dma((3,)), dma, dma((3,)), dma, dma((3, 2)), dma((NX, 2)), dma, dma((2, 3)),
            dma, dma((3, 2)), dma((3,)), dma, dma((3,)), dma, dma((3,)), dma, dma((3,)), dma, dma((3,)),
            dma, dma((2, 2)), dma((2,)), dma((2,)),
        ],
        compiler_params=pltpu.CompilerParams(
            collective_id=0, has_side_effects=True, vmem_limit_bytes=56 << 20
        ),
    )(key_tokens, value_tokens, queries, token_rate.reshape(1, TOK), fast_weights)


def solution(mesh):
    rows = P(("grp", "dev"), None)
    in_specs = (rows, rows, rows, P(("grp", "dev")), P(None, ("grp", "dev"), None))
    return jax.shard_map(body, mesh=mesh, in_specs=in_specs, out_specs=rows, check_vma=False)
```
